512 devices in a mesh: sect: 2 (over core), grp: 64 (over y, z), tp: 4 (over x).
Axes of the slice: x: 4, y: 8, z: 8, core: 2. Of those that a mesh axis runs over, the one named last changes fastest.
Arguments:
- keys: bfloat16 [256, 256, 4096], P(('sect', 'grp'), 'tp'), may hold values from -4 to 4
- values: bfloat16 [256, 256, 4096], P(('sect', 'grp'), 'tp'), may hold values from -4 to 4
- frozen_query_projection: bfloat16 [8, 256, 4096], P('sect', None, 'grp'), may hold values from -32 to 32
- context_gradient: bfloat16 [8, 256, 4096], P('sect', None, 'grp'), may hold values from -48 to 48
- hidden: bfloat16 [8, 256, 4096], P('sect', None, 'grp'), may hold values from -6 to 6
- adapter_down_weight: bfloat16 [4096, 64], P('grp'), may hold values from -0.09375 to 0.09375
- adapter_up_weight: bfloat16 [64, 4096], P(None, 'grp'), may hold values from -0.09375 to 0.09375
- owner: int32 [256], P(('sect', 'grp')), may hold values from 0 to 4, as said below
- counts: int32 [128], P(('sect', 'grp')), may hold values from 1 to 2, as said below
- target_length: int32 [8], P('sect'), may hold values from 64 to 256
Outputs:
- adapted_query_gradient: bfloat16 [8, 256, 4096], P('sect', 'tp', 'grp')
- grad_keys: bfloat16 [256, 256, 4096], P(('sect', 'grp'), 'tp')
- grad_values: bfloat16 [256, 256, 4096], P(('sect', 'grp'), 'tp')
- grad_a: float32 [4096, 64], P('grp')
- grad_b: float32 [64, 4096], P(None, 'grp')
The draws below stay inside these ranges and needn't reach their ends.
Inputs may be any that keep to these rules, and one draw needn't show every extreme that they name: `owner`: for live slots, the question among the 4 of the same half that reads the passage; every question is named by exactly 28 live slots; empty slots hold 4. `counts`: in each aligned block of four devices of a half exactly one device has 1 live slots and the others 2; live slots are the first ones of a device.
All inputs are finite; a program needn't handle non-finite values.
Results may differ from the reference program's by a relative error of at most 0.017.
The reference program's roundings to bfloat16 on the way count: a program that leaves them out, or rounds other values in their place, can miss the bound.
Values may be sent and summed in bfloat16 or wider, within the bound.
No kernel may reach another device: no remote copies, remote signals or barrier semaphores. Data moves between devices by JAX's collectives and lax.ppermute only.
A program may use at most 64 MiB of HBM per device.

```python
import jax
import jax.numpy as jnp
from jax import lax

MODEL_WIDTH = 4096
ATTENTION_HEADS = 64
HEAD_DIMENSION = 64
ADAPTER_RANK = 64
L = 256
P_CAP = 2
TGT = 256
QH = 4
PPQ = 28
QUESTIONS = 8
SLOTS = 256
N_SECT = 2
N_GRP = 64


def layout_draw(key):
    key = jax.random.fold_in(key, 11)
    half_slots = P_CAP * N_GRP

    def one_half(half_key):
        key_one, key_two = jax.random.split(half_key, 2)
        single = jax.random.randint(key_one, (N_GRP // 4,), 0, 4)
        device = jnp.arange(N_GRP, dtype=jnp.int32)
        counts = P_CAP - (device % 4 == jnp.repeat(single, 4)).astype(jnp.int32)
        position = jnp.arange(half_slots, dtype=jnp.int32) % P_CAP
        live = position < jnp.repeat(counts, P_CAP)
        shuffled = jax.random.permutation(key_two, half_slots).astype(jnp.int32)
        sort_key = jnp.where(live, shuffled, shuffled + half_slots)
        order = jnp.argsort(sort_key).astype(jnp.int32)
        ranks = jnp.zeros((half_slots,), jnp.int32).at[order].set(jnp.arange(half_slots, dtype=jnp.int32))
        owner = jnp.where(live, ranks // PPQ, QH).astype(jnp.int32)
        return (counts.astype(jnp.int32), owner)
    half_keys = jax.random.split(key, N_SECT)
    counts, owner = jax.vmap(one_half)(half_keys)
    return (counts.reshape(-1), owner.reshape(-1))


def draw_keys(key, part):
    rest_key = jax.random.fold_in(key, 29)
    trailing = jax.random.truncated_normal(rest_key, -4.0, 4.0, (SLOTS, L, ATTENTION_HEADS * HEAD_DIMENSION), jnp.float32)
    drawn = trailing
    return drawn.astype(jnp.bfloat16)


def draw_frozen_query_projection(key, part):
    base_key = jax.random.fold_in(key, 31)
    shape = (QUESTIONS, TGT, ATTENTION_HEADS * HEAD_DIMENSION)
    base = 0.15 * jax.random.truncated_normal(base_key, -6.0, 6.0, shape, jnp.float32)
    return base.astype(jnp.bfloat16)


def draw_owner(key, part):
    return layout_draw(key)[1]


def draw_counts(key, part):
    return layout_draw(key)[0]


def draw_target_length(key, part):
    key = jax.random.fold_in(key, 5)
    key_one, key_two = jax.random.split(key)
    lengths = jax.random.randint(key_one, (QUESTIONS,), TGT // 4, TGT + 1)
    longest = jax.random.randint(key_two, (), 0, QUESTIONS)
    return lengths.at[longest].set(TGT).astype(jnp.int32)


def block_scale(stream_key, shape, cuts, low, high):
    gain = 1.0
    for dim, shards_of in cuts:
        heights = jax.random.uniform(jax.random.fold_in(jax.random.fold_in(stream_key, 6), dim), (shards_of,), jnp.float32, low / len(cuts), high / len(cuts))
        gain = gain * jnp.repeat(jnp.exp(heights), shape[dim] // shards_of).reshape((-1,) + (1,) * (len(shape) - 1 - dim))
    return gain


def noise(own_key, dims, deviation, limit, cuts=(), kind=jnp.bfloat16):
    level = block_scale(own_key, dims, cuts, -0.22, 0.18) if cuts else 1.0
    entries = jax.random.normal(own_key, dims, jnp.float32) * deviation * level
    return jnp.minimum(jnp.maximum(entries, -limit), limit).astype(kind)


def setup_inputs(seed: int = 0) -> dict:
    seeds = jax.random.split(jax.random.key(seed), 11)
    keys = draw_keys(jax.random.fold_in(seeds[10], 71), 0)
    values = noise(seeds[1], (SLOTS, L, ATTENTION_HEADS * HEAD_DIMENSION), 1.0, 4.0, ((0, 128), (1, 4)))
    frozen_query_projection = draw_frozen_query_projection(jax.random.fold_in(seeds[10], 71), 0)
    context_gradient = noise(seeds[3], (QUESTIONS, TGT, ATTENTION_HEADS * HEAD_DIMENSION), 8.0, 48.0, ((0, 2), (2, 64)))
    hidden = noise(seeds[4], (QUESTIONS, TGT, MODEL_WIDTH), 1.0, 6.0, ((0, 2), (2, 64)))
    adapter_down_weight = noise(seeds[5], (MODEL_WIDTH, ADAPTER_RANK), MODEL_WIDTH ** -0.5, 0.09375, ((0, 64),))
    adapter_up_weight = noise(seeds[6], (ADAPTER_RANK, ATTENTION_HEADS * HEAD_DIMENSION), (64 * ADAPTER_RANK) ** -0.5, 0.09375, ((1, 64),))
    owner = draw_owner(jax.random.fold_in(seeds[10], 71), 0)
    counts = draw_counts(jax.random.fold_in(seeds[10], 71), 0)
    target_length = draw_target_length(jax.random.fold_in(seeds[10], 71), 0)
    return {"keys": keys, "values": values, "frozen_query_projection": frozen_query_projection, "context_gradient": context_gradient, "hidden": hidden, "adapter_down_weight": adapter_down_weight, "adapter_up_weight": adapter_up_weight, "owner": owner, "counts": counts, "target_length": target_length}


def passage_order(owner_all, counts_all, questions, per_question):
    slot_count = owner_all.shape[0]
    per_device = slot_count // counts_all.shape[0]
    position = jnp.arange(slot_count, dtype=jnp.int32) % per_device
    live = position < jnp.repeat(counts_all, per_device)
    sort_key = jnp.where(live, owner_all, questions).astype(jnp.int32)
    order = jnp.argsort(sort_key, stable=True).astype(jnp.int32)
    return order[: questions * per_question].reshape(questions, per_question)


def attend_head(pieces):
    query_head, key_head, value_head, grad_head = pieces
    scores = jnp.dot(query_head, key_head.T, preferred_element_type=jnp.float32)
    row_top = jnp.max(scores, axis=1, keepdims=True)
    exp_scores = jnp.exp(scores - row_top)
    weights = exp_scores / jnp.sum(exp_scores, axis=1, keepdims=True)
    weights_low = weights.astype(jnp.bfloat16)
    attended = jnp.dot(weights_low, value_head, preferred_element_type=jnp.float32)
    delta = jnp.sum(grad_head.astype(jnp.float32) * attended, axis=1, keepdims=True)
    prob_grad = jnp.dot(grad_head, value_head.T, preferred_element_type=jnp.float32)
    score_grad = (weights * (prob_grad - delta)).astype(jnp.bfloat16)
    query_grad = jnp.dot(score_grad, key_head, preferred_element_type=jnp.float32)
    key_grad = jnp.dot(score_grad.T, query_head, preferred_element_type=jnp.float32).astype(jnp.bfloat16)
    value_grad = jnp.dot(weights_low.T, grad_head, preferred_element_type=jnp.float32).astype(jnp.bfloat16)
    return query_grad, key_grad, value_grad


def reference(keys, values, frozen_query_projection, context_gradient, hidden, adapter_down_weight, adapter_up_weight, owner, counts, target_length):
    width = ATTENTION_HEADS * HEAD_DIMENSION
    adapter_latent = jnp.dot(hidden.reshape(-1, MODEL_WIDTH), adapter_down_weight, preferred_element_type=jnp.float32).astype(jnp.bfloat16)
    raised_latent = jnp.dot(adapter_latent, adapter_up_weight, preferred_element_type=jnp.float32)
    query = (frozen_query_projection.reshape(-1, width).astype(jnp.float32) + raised_latent).astype(jnp.bfloat16)
    query = query.reshape(QUESTIONS, TGT, ATTENTION_HEADS, HEAD_DIMENSION)
    step_ids = lax.broadcasted_iota(jnp.int32, (QUESTIONS, TGT), 1)
    keep = step_ids < target_length[:, None]
    upstream = jnp.where(keep[:, :, None], context_gradient, jnp.zeros_like(context_gradient))
    upstream = upstream.reshape(QUESTIONS, TGT, ATTENTION_HEADS, HEAD_DIMENSION)
    half_slots = P_CAP * N_GRP
    query_grads = []
    slot_lists = []
    key_grads = []
    value_grads = []
    for half_index in range(N_SECT):
        chosen = passage_order(owner[half_index * half_slots:(half_index + 1) * half_slots],
                               counts[half_index * N_GRP:(half_index + 1) * N_GRP], QH, PPQ)
        for question in range(QH):
            which = half_index * QH + question
            slot_ids = chosen[question] + half_index * half_slots
            key_rows = keys[slot_ids].reshape(PPQ * L, ATTENTION_HEADS, HEAD_DIMENSION).transpose(1, 0, 2)
            value_rows = values[slot_ids].reshape(PPQ * L, ATTENTION_HEADS, HEAD_DIMENSION).transpose(1, 0, 2)
            outcome = lax.map(attend_head, (query[which].transpose(1, 0, 2), key_rows, value_rows,
                                            upstream[which].transpose(1, 0, 2)))
            query_grads.append(outcome[0].transpose(1, 0, 2).reshape(TGT, width))
            key_grads.append(outcome[1].transpose(1, 0, 2).reshape(PPQ, L, width))
            value_grads.append(outcome[2].transpose(1, 0, 2).reshape(PPQ, L, width))
            slot_lists.append(slot_ids)
    adapted_query_gradient = jnp.stack(query_grads).astype(jnp.bfloat16)
    all_slots = jnp.concatenate(slot_lists).astype(jnp.int32)
    grad_keys = jnp.zeros((SLOTS, L, width), jnp.bfloat16).at[all_slots].set(jnp.concatenate(key_grads))
    grad_values = jnp.zeros((SLOTS, L, width), jnp.bfloat16).at[all_slots].set(jnp.concatenate(value_grads))
    flattened_gradient = adapted_query_gradient.reshape(-1, width)
    adapter_latent_gradient = jnp.dot(flattened_gradient, adapter_up_weight.T, preferred_element_type=jnp.float32).astype(jnp.bfloat16)
    grad_a = jnp.dot(hidden.reshape(-1, MODEL_WIDTH).T, adapter_latent_gradient, preferred_element_type=jnp.float32)
    grad_b = jnp.dot(adapter_latent.T, flattened_gradient, preferred_element_type=jnp.float32)
    return adapted_query_gradient, grad_keys, grad_values, grad_a, grad_b
```

```python
import functools

import jax
import jax.numpy as jnp
from jax import lax
from jax.experimental import pallas as pl
from jax.experimental.pallas import tpu as pltpu
from jax.sharding import PartitionSpec as P

HEAD = 64
BF16 = jnp.bfloat16
F32 = jnp.float32
VMEM_LIMIT = 32 * 1024 * 1024


def pack_kernel(k_ref, v_ref, o_ref):
    slots, span, width = k_ref.shape
    for pair in range(width // (2 * HEAD)):
        low = pair * 2 * HEAD
        for slot in range(slots):
            rows = pl.ds(slot * span, span)
            k = k_ref[slot, :, low : low + 2 * HEAD]
            v = v_ref[slot, :, low : low + 2 * HEAD]
            o_ref[2 * pair, rows, :] = jnp.concatenate([k[:, :HEAD], v[:, :HEAD]], axis=1)
            o_ref[2 * pair + 1, rows, :] = jnp.concatenate([k[:, HEAD:], v[:, HEAD:]], axis=1)


def unpack_kernel(i_ref, k_ref, v_ref):
    slots, span, width = k_ref.shape
    for pair in range(width // (2 * HEAD)):
        low = pair * 2 * HEAD
        for slot in range(slots):
            rows = pl.ds(slot * span, span)
            even = i_ref[2 * pair, rows, :]
            odd = i_ref[2 * pair + 1, rows, :]
            k_ref[slot, :, low : low + 2 * HEAD] = jnp.concatenate([even[:, :HEAD], odd[:, :HEAD]], axis=1)
            v_ref[slot, :, low : low + 2 * HEAD] = jnp.concatenate([even[:, HEAD:], odd[:, HEAD:]], axis=1)


PACK_HEADS = 16


def pack(keys, values):
    slots, span, width = keys.shape
    heads = width // HEAD
    part = pl.BlockSpec((slots, span, PACK_HEADS * HEAD), lambda i: (0, 0, i))
    return pl.pallas_call(
        pack_kernel,
        grid=(heads // PACK_HEADS,),
        in_specs=[part, part],
        out_specs=pl.BlockSpec((PACK_HEADS, slots * span, 2 * HEAD), lambda i: (i, 0, 0)),
        out_shape=jax.ShapeDtypeStruct((heads, slots * span, 2 * HEAD), keys.dtype),
        compiler_params=pltpu.CompilerParams(vmem_limit_bytes=VMEM_LIMIT),
        cost_estimate=pl.CostEstimate(flops=0, bytes_accessed=8 * slots * span * width, transcendentals=0),
        name="pack",
    )(keys, values)


def unpack(table, slots):
    heads, rows, _ = table.shape
    span = rows // slots
    part = pl.BlockSpec((slots, span, PACK_HEADS * HEAD), lambda i: (0, 0, i))
    shape = jax.ShapeDtypeStruct((slots, span, heads * HEAD), table.dtype)
    return pl.pallas_call(
        unpack_kernel,
        grid=(heads // PACK_HEADS,),
        in_specs=[pl.BlockSpec((PACK_HEADS, rows, 2 * HEAD), lambda i: (i, 0, 0))],
        out_specs=[part, part],
        out_shape=[shape, shape],
        compiler_params=pltpu.CompilerParams(vmem_limit_bytes=VMEM_LIMIT),
        cost_estimate=pl.CostEstimate(flops=0, bytes_accessed=8 * slots * span * heads * HEAD, transcendentals=0),
        name="unpack",
    )(table)


CHUNK_SLOTS = 4


def two_sided(q_ref, u_ref):
    q, u = q_ref[0], u_ref[0]
    zero = jnp.zeros_like(q)
    return jnp.concatenate(
        [jnp.concatenate([q, zero], axis=1), jnp.concatenate([zero, u], axis=1)], axis=0
    )


def gathered(chosen_ref, t_ref, question, per_question, chunk):
    return jnp.concatenate(
        [
            t_ref[chosen_ref[question * per_question + chunk * CHUNK_SLOTS + i]]
            for i in range(CHUNK_SLOTS)
        ],
        axis=0,
    )


def stats_kernel(per_question, chosen_ref, q_ref, u_ref, t_ref, o_ref):
    question = pl.program_id(0)
    targets = q_ref.shape[2]
    both = two_sided(q_ref, u_ref)
    top = jnp.full((1, targets), -jnp.inf, F32)
    mass = jnp.zeros((1, targets), F32)
    dot = jnp.zeros((1, targets), F32)
    for chunk in range(per_question // CHUNK_SLOTS):
        rows = gathered(chosen_ref, t_ref, question, per_question, chunk)
        prod = jnp.dot(rows, both, preferred_element_type=F32)
        scores, prob_grad = prod[:, :targets], prod[:, targets:]
        new_top = jnp.maximum(top, jnp.max(scores, axis=0, keepdims=True))
        scale = jnp.exp(top - new_top)
        exp_scores = jnp.exp(scores - new_top)
        mass = mass * scale + jnp.sum(exp_scores, axis=0, keepdims=True)
        dot = dot * scale + jnp.sum(exp_scores * prob_grad, axis=0, keepdims=True)
        top = new_top
    o_ref[0] = jnp.concatenate([top, mass, dot, jnp.zeros((5, targets), F32)], axis=0)


def grad_kernel(per_question, chosen_ref, q_ref, u_ref, s_ref, t_ref, dq_ref, o_ref):
    question = pl.program_id(0)
    targets = q_ref.shape[2]
    peers, _, pair_width = dq_ref.shape
    piece = targets // peers

    @pl.when(question == 0)
    def _():
        o_ref[...] = jnp.zeros_like(o_ref)

    both = two_sided(q_ref, u_ref)
    top, inverse, delta = s_ref[0, 0:1, :], s_ref[0, 1:2, :], s_ref[0, 2:3, :]
    dq = jnp.zeros((2 * HEAD, targets), F32)
    for chunk in range(per_question // CHUNK_SLOTS):
        rows = gathered(chosen_ref, t_ref, question, per_question, chunk)
        span = t_ref.shape[1]
        prod = jnp.dot(rows, both, preferred_element_type=F32)
        scores, prob_grad = prod[:, :targets], prod[:, targets:]
        weights = jnp.exp(scores - top) * inverse
        score_grad = (weights * (prob_grad - delta)).astype(BF16)
        pair = jnp.concatenate([score_grad, weights.astype(BF16)], axis=1)
        out = lax.dot_general(
            pair, both, (((1,), (1,)), ((), ())), preferred_element_type=F32
        ).astype(BF16)
        for i in range(CHUNK_SLOTS):
            o_ref[chosen_ref[question * per_question + chunk * CHUNK_SLOTS + i]] = out[
                i * span : (i + 1) * span
            ]
        dq = dq + lax.dot_general(
            rows, score_grad, (((0,), (0,)), ((), ())), preferred_element_type=F32
        )

    for side in range(pair_width // piece):

        @pl.when(question % (pair_width // piece) == side)
        def _():
            for peer in range(peers):
                dq_ref[peer, :, side * piece : (side + 1) * piece] = dq[
                    :HEAD, peer * piece : (peer + 1) * piece
                ]


def attend_stats(chosen, query_t, upstream_t, table, per_question):
    questions, size, targets = query_t.shape
    one = pl.BlockSpec((1, size, targets), lambda q, c: (q, 0, 0))
    whole = pl.BlockSpec(table.shape, lambda q, c: (0, 0, 0))
    keys = per_question * table.shape[1]
    return pl.pallas_call(
        functools.partial(stats_kernel, per_question),
        grid_spec=pltpu.PrefetchScalarGridSpec(
            num_scalar_prefetch=1,
            grid=(questions,),
            in_specs=[one, one, whole],
            out_specs=pl.BlockSpec((1, 8, targets), lambda q, c: (q, 0, 0)),
        ),
        out_shape=jax.ShapeDtypeStruct((questions, 8, targets), F32),
        compiler_params=pltpu.CompilerParams(vmem_limit_bytes=VMEM_LIMIT),
        cost_estimate=pl.CostEstimate(
            flops=8 * questions * targets * keys * HEAD,
            bytes_accessed=2 * table.size,
            transcendentals=questions * targets * keys,
        ),
        name="stats",
    )(chosen, query_t, upstream_t, table)


def attend_grads(chosen, query_t, upstream_t, stats, table, per_question, peers):
    questions, size, targets = query_t.shape
    one = pl.BlockSpec((1, size, targets), lambda q, c: (q, 0, 0))
    whole = pl.BlockSpec(table.shape, lambda q, c: (0, 0, 0))
    keys = per_question * table.shape[1]
    piece = targets // peers
    in_block = 128 // piece
    return pl.pallas_call(
        functools.partial(grad_kernel, per_question),
        grid_spec=pltpu.PrefetchScalarGridSpec(
            num_scalar_prefetch=1,
            grid=(questions,),
            in_specs=[one, one, pl.BlockSpec((1, 8, targets), lambda q, c: (q, 0, 0)), whole],
            out_specs=[
                pl.BlockSpec((peers, HEAD, 128), lambda q, c: (0, 0, q // in_block)),
                whole,
            ],
        ),
        out_shape=[
            jax.ShapeDtypeStruct((peers, HEAD, questions * piece), F32),
            jax.ShapeDtypeStruct(table.shape, BF16),
        ],
        compiler_params=pltpu.CompilerParams(vmem_limit_bytes=VMEM_LIMIT),
        cost_estimate=pl.CostEstimate(
            flops=24 * questions * targets * keys * HEAD,
            bytes_accessed=4 * table.size,
            transcendentals=questions * targets * keys,
        ),
        name="grads",
    )(chosen, query_t, upstream_t, stats, table)


def swap_sum(x, axis, shift, radix):
    size = lax.axis_size(axis)
    got = [x] + [
        lax.ppermute(x, axis, [(i, i ^ (k << shift)) for i in range(size)]) for k in range(1, radix)
    ]
    while len(got) > 1:
        got = [a + b for a, b in zip(got[0::2], got[1::2])]
    return got[0]


def group_sum(x):
    size, shift = lax.axis_size("grp"), 0
    while (1 << shift) < size:
        radix = min(4, size >> shift)
        x = swap_sum(x, "grp", shift, radix)
        shift += radix.bit_length() - 1
    return x


def gather_tp(x):
    size, here = lax.axis_size("tp"), lax.axis_index("tp")
    got = [x] + [
        lax.ppermute(x, "tp", [(i, (i + k) % size) for i in range(size)]) for k in range(1, size)
    ]
    order = (here - jnp.arange(size, dtype=jnp.int32)) % size
    return jnp.stack(got)[order]


def scatter_sum_tp(x):
    size, here = lax.axis_size("tp"), lax.axis_index("tp")
    own = lax.dynamic_index_in_dim(x, here, 0, keepdims=False)
    for k in range(1, size):
        sent = lax.dynamic_index_in_dim(x, (here + k) % size, 0, keepdims=False)
        own = own + lax.ppermute(sent, "tp", [(i, (i + k) % size) for i in range(size)])
    return own


def local(
    keys,
    values,
    frozen_query_projection,
    context_gradient,
    hidden,
    adapter_down_weight,
    adapter_up_weight,
    owner,
    counts,
    target_length,
):
    group_count, token_split = lax.axis_size("grp"), lax.axis_size("tp")
    questions, targets, _ = frozen_query_projection.shape
    slots_dev, span, _ = keys.shape
    total_slots = group_count * slots_dev
    per_question = (total_slots - group_count // 4) // questions
    piece = targets // token_split

    packed = pack(keys, values)
    table = lax.all_to_all(packed, "grp", split_axis=0, concat_axis=0, tiled=True)
    table = table.reshape(total_slots, span, 2 * HEAD)

    start = lax.axis_index("tp") * piece
    hidden_t = jnp.swapaxes(hidden, 1, 2)
    hidden_cut = lax.dynamic_slice_in_dim(hidden_t, start, piece, 2)
    hidden_cut = jnp.transpose(hidden_cut, (1, 0, 2)).reshape(HEAD, questions * piece)
    latent_part = lax.dot_general(
        adapter_down_weight, hidden_cut, (((0,), (0,)), ((), ())), preferred_element_type=F32
    )
    live = jnp.arange(slots_dev, dtype=jnp.int32) < counts[0]
    tag = jnp.where(live, owner, questions).astype(F32)
    own_slots = lax.axis_index("grp") * slots_dev
    tag_row = jnp.zeros((questions * piece,), F32)
    tag_row = lax.dynamic_update_slice(tag_row, tag, (own_slots,))
    tags = jnp.pad(tag_row[None], ((0, 7), (0, 0)))
    summed = group_sum(jnp.concatenate([latent_part, tags], axis=0))
    latent_cut = summed[:HEAD].astype(BF16)

    slot_key = summed[HEAD, :total_slots].astype(jnp.int32)
    slot_ids = jnp.arange(total_slots, dtype=jnp.int32)
    same = (slot_key[:, None] == slot_key[None, :]) & (slot_ids[None, :] < slot_ids[:, None])
    rank = jnp.sum(same.astype(jnp.int32), axis=1)
    place = slot_key * per_question + rank
    wanted = jnp.arange(questions * per_question, dtype=jnp.int32)
    hit = (place[None, :] == wanted[:, None]) & (slot_key < questions)[None, :]
    chosen = jnp.sum(jnp.where(hit, slot_ids[None, :], 0), axis=1)

    latent_all = gather_tp(latent_cut).reshape(token_split, HEAD, questions, piece)
    latent_t = jnp.transpose(latent_all, (2, 1, 0, 3)).reshape(questions, HEAD, targets)
    raised = jnp.einsum("rd,qrt->qdt", adapter_up_weight, latent_t, preferred_element_type=F32)
    frozen_t = jnp.swapaxes(frozen_query_projection, 1, 2)
    query_t = (frozen_t.astype(F32) + raised).astype(BF16)
    step_ids = lax.broadcasted_iota(jnp.int32, (questions, 1, targets), 2)
    keep = step_ids < target_length[:, None, None]
    upstream_t = jnp.swapaxes(context_gradient, 1, 2)
    upstream_t = jnp.where(keep, upstream_t, jnp.zeros_like(upstream_t))

    stats = attend_stats(chosen, query_t, upstream_t, table, per_question)
    size = lax.axis_size("tp")
    parts = [stats] + [
        lax.ppermute(stats, "tp", [(i, i ^ k) for i in range(size)]) for k in range(1, size)
    ]
    tops = [p[:, 0] for p in parts]
    top = functools.reduce(jnp.maximum, tops)
    scales = [jnp.exp(t - top) for t in tops]
    mass = sum(p[:, 1] * s for p, s in zip(parts, scales))
    inverse = 1.0 / mass
    delta = sum(p[:, 2] * s for p, s in zip(parts, scales)) * inverse
    zeros = jnp.zeros_like(top)
    row_stats = jnp.stack([top, inverse, delta] + [zeros] * 5, axis=1)

    dq_parts, grad_table = attend_grads(
        chosen, query_t, upstream_t, row_stats, table, per_question, token_split
    )
    back = lax.all_to_all(
        grad_table.reshape(group_count, slots_dev * span, 2 * HEAD),
        "grp",
        split_axis=0,
        concat_axis=0,
        tiled=True,
    )
    grad_keys, grad_values = unpack(back, slots_dev)

    dq_t = scatter_sum_tp(dq_parts).astype(BF16)
    adapted = jnp.transpose(dq_t.reshape(HEAD, questions, piece), (1, 2, 0))
    latent_grad_part = jnp.dot(adapter_up_weight, dq_t, preferred_element_type=F32)
    latent_grad = group_sum(latent_grad_part).astype(BF16)
    last = (((1,), (1,)), ((), ()))
    grad_a = lax.dot_general(hidden_cut, latent_grad, last, preferred_element_type=F32)
    grad_b = lax.dot_general(latent_cut, dq_t, last, preferred_element_type=F32)
    both = jnp.concatenate([grad_a, grad_b], axis=1)
    both = swap_sum(swap_sum(both, "tp", 0, token_split), "sect", 0, lax.axis_size("sect"))
    return (adapted, grad_keys, grad_values, both[:, :HEAD], both[:, HEAD:])


def solution(mesh):
    return jax.shard_map(
        local,
        mesh=mesh,
        in_specs=(
            P(("sect", "grp"), "tp", None),
            P(("sect", "grp"), "tp", None),
            P("sect", None, "grp"),
            P("sect", None, "grp"),
            P("sect", None, "grp"),
            P("grp", None),
            P(None, "grp"),
            P(("sect", "grp")),
            P(("sect", "grp")),
            P("sect"),
        ),
        out_specs=(
            P("sect", "tp", "grp"),
            P(("sect", "grp"), "tp", None),
            P(("sect", "grp"), "tp", None),
            P("grp", None),
            P(None, "grp"),
        ),
        check_vma=False,
    )
```

```python
import functools

import jax
import jax.numpy as jnp
from jax import lax
from jax.experimental import pallas as pl
from jax.experimental.pallas import tpu as pltpu
from jax.sharding import PartitionSpec as P

HEAD = 64
BF16 = jnp.bfloat16
F32 = jnp.float32
VMEM_LIMIT = 32 * 1024 * 1024


def pack_kernel(k_ref, v_ref, o_ref):
    slots, span, width = k_ref.shape
    for pair in range(width // (2 * HEAD)):
        low = pair * 2 * HEAD
        for slot in range(slots):
            rows = pl.ds(slot * span, span)
            k = k_ref[slot, :, low : low + 2 * HEAD]
            v = v_ref[slot, :, low : low + 2 * HEAD]
            o_ref[2 * pair, rows, :] = jnp.concatenate([k[:, :HEAD], v[:, :HEAD]], axis=1)
            o_ref[2 * pair + 1, rows, :] = jnp.concatenate([k[:, HEAD:], v[:, HEAD:]], axis=1)


def unpack_kernel(i_ref, k_ref, v_ref):
    slots, span, width = k_ref.shape
    for pair in range(width // (2 * HEAD)):
        low = pair * 2 * HEAD
        for slot in range(slots):
            rows = pl.ds(slot * span, span)
            even = i_ref[2 * pair, rows, :]
            odd = i_ref[2 * pair + 1, rows, :]
            k_ref[slot, :, low : low + 2 * HEAD] = jnp.concatenate([even[:, :HEAD], odd[:, :HEAD]], axis=1)
            v_ref[slot, :, low : low + 2 * HEAD] = jnp.concatenate([even[:, HEAD:], odd[:, HEAD:]], axis=1)


PACK_HEADS = 16


def pack(keys, values, spare):
    slots, span, width = keys.shape
    heads, rows = width // HEAD, slots * span + spare
    part = pl.BlockSpec((slots, span, PACK_HEADS * HEAD), lambda i: (0, 0, i))
    return pl.pallas_call(
        pack_kernel,
        grid=(heads // PACK_HEADS,),
        in_specs=[part, part],
        out_specs=pl.BlockSpec((PACK_HEADS, rows, 2 * HEAD), lambda i: (i, 0, 0)),
        out_shape=jax.ShapeDtypeStruct((heads, rows, 2 * HEAD), keys.dtype),
        compiler_params=pltpu.CompilerParams(vmem_limit_bytes=VMEM_LIMIT),
        cost_estimate=pl.CostEstimate(flops=0, bytes_accessed=8 * slots * span * width, transcendentals=0),
        name="pack",
    )(keys, values)


def unpack(table, slots, span):
    heads, rows, _ = table.shape
    part = pl.BlockSpec((slots, span, PACK_HEADS * HEAD), lambda i: (0, 0, i))
    shape = jax.ShapeDtypeStruct((slots, span, heads * HEAD), table.dtype)
    return pl.pallas_call(
        unpack_kernel,
        grid=(heads // PACK_HEADS,),
        in_specs=[pl.BlockSpec((PACK_HEADS, rows, 2 * HEAD), lambda i: (i, 0, 0))],
        out_specs=[part, part],
        out_shape=[shape, shape],
        compiler_params=pltpu.CompilerParams(vmem_limit_bytes=VMEM_LIMIT),
        cost_estimate=pl.CostEstimate(flops=0, bytes_accessed=8 * slots * span * heads * HEAD, transcendentals=0),
        name="unpack",
    )(table)


CHUNK_SLOTS = 4


def two_sided(q_ref, u_ref):
    q, u = q_ref[0], u_ref[0]
    zero = jnp.zeros_like(q)
    return jnp.concatenate(
        [jnp.concatenate([q, zero], axis=1), jnp.concatenate([zero, u], axis=1)], axis=0
    )


def slot_rows(chosen_ref, slots, span, entry):
    slot = chosen_ref[entry]
    return slot // slots, pl.ds(pl.multiple_of(lax.rem(slot, slots) * span, span), span)


def gathered(chosen_ref, t_ref, slots, span, first):
    blocks = []
    for i in range(CHUNK_SLOTS):
        device, rows = slot_rows(chosen_ref, slots, span, first + i)
        blocks.append(t_ref[device, rows, :])
    return jnp.concatenate(blocks, axis=0)


def stats_kernel(per_question, slots, span, chosen_ref, q_ref, u_ref, t_ref, o_ref):
    question = pl.program_id(0)
    targets = q_ref.shape[2]
    both = two_sided(q_ref, u_ref)
    top = jnp.full((1, targets), -jnp.inf, F32)
    mass = jnp.zeros((1, targets), F32)
    dot = jnp.zeros((1, targets), F32)
    for chunk in range(per_question // CHUNK_SLOTS):
        first = question * per_question + chunk * CHUNK_SLOTS
        rows = gathered(chosen_ref, t_ref, slots, span, first)
        prod = jnp.dot(rows, both, preferred_element_type=F32)
        scores, prob_grad = prod[:, :targets], prod[:, targets:]
        new_top = jnp.maximum(top, jnp.max(scores, axis=0, keepdims=True))
        scale = jnp.exp(top - new_top)
        exp_scores = jnp.exp(scores - new_top)
        mass = mass * scale + jnp.sum(exp_scores, axis=0, keepdims=True)
        dot = dot * scale + jnp.sum(exp_scores * prob_grad, axis=0, keepdims=True)
        top = new_top
    o_ref[0] = jnp.concatenate([top, mass, dot, jnp.zeros((5, targets), F32)], axis=0)


def row_stats(s_ref):
    members = s_ref.shape[0]
    tops = [s_ref[i, 0, 0:1, :] for i in range(members)]
    top = functools.reduce(jnp.maximum, tops)
    scales = [jnp.exp(t - top) for t in tops]
    inverse = 1.0 / sum(s_ref[i, 0, 1:2, :] * scales[i] for i in range(members))
    delta = sum(s_ref[i, 0, 2:3, :] * scales[i] for i in range(members)) * inverse
    return top, inverse, delta


def grad_kernel(
    per_question, slots, span, chosen_ref, q_ref, u_ref, w_ref, s_ref, t_ref, dq_ref, l_ref, o_ref
):
    question = pl.program_id(0)
    targets = q_ref.shape[2]
    peers, _, pair_width = dq_ref.shape
    piece = targets // peers

    @pl.when(question == 0)
    def _():
        o_ref[...] = jnp.zeros_like(o_ref)

    both = two_sided(q_ref, u_ref)
    top, inverse, delta = row_stats(s_ref)
    dq = jnp.zeros((2 * HEAD, targets), F32)
    for chunk in range(per_question // CHUNK_SLOTS):
        first = question * per_question + chunk * CHUNK_SLOTS
        rows = gathered(chosen_ref, t_ref, slots, span, first)
        prod = jnp.dot(rows, both, preferred_element_type=F32)
        scores, prob_grad = prod[:, :targets], prod[:, targets:]
        weights = jnp.exp(scores - top) * inverse
        score_grad = (weights * (prob_grad - delta)).astype(BF16)
        pair = jnp.concatenate([score_grad, weights.astype(BF16)], axis=1)
        out = lax.dot_general(
            pair, both, (((1,), (1,)), ((), ())), preferred_element_type=F32
        ).astype(BF16)
        for i in range(CHUNK_SLOTS):
            device, place = slot_rows(chosen_ref, slots, span, first + i)
            o_ref[device, place, :] = out[i * span : (i + 1) * span]
        dq = dq + lax.dot_general(
            rows, score_grad, (((0,), (0,)), ((), ())), preferred_element_type=F32
        )
    dq = dq[:HEAD]

    for side in range(pair_width // piece):

        @pl.when(question % (pair_width // piece) == side)
        def _():
            for peer in range(peers):
                dq_ref[peer, :, side * piece : (side + 1) * piece] = dq[
                    :, peer * piece : (peer + 1) * piece
                ]

    high = dq.astype(BF16)
    low = (dq - high.astype(F32)).astype(BF16)
    latent = jnp.dot(w_ref[...], high, preferred_element_type=F32) + jnp.dot(
        w_ref[...], low, preferred_element_type=F32
    )
    lanes = l_ref.shape[2]
    for part in range(targets // lanes):
        row = question * (targets // lanes) + part
        l_ref[:, pl.ds(row, 1), :] = latent[:, None, part * lanes : (part + 1) * lanes]


def attend_stats(chosen, query_t, upstream_t, table, per_question, slots, span):
    questions, size, targets = query_t.shape
    one = pl.BlockSpec((1, size, targets), lambda q, c: (q, 0, 0))
    whole = pl.BlockSpec(table.shape, lambda q, c: (0, 0, 0))
    keys = per_question * span
    return pl.pallas_call(
        functools.partial(stats_kernel, per_question, slots, span),
        grid_spec=pltpu.PrefetchScalarGridSpec(
            num_scalar_prefetch=1,
            grid=(questions,),
            in_specs=[one, one, whole],
            out_specs=pl.BlockSpec((1, 8, targets), lambda q, c: (q, 0, 0)),
        ),
        out_shape=jax.ShapeDtypeStruct((questions, 8, targets), F32),
        compiler_params=pltpu.CompilerParams(vmem_limit_bytes=VMEM_LIMIT),
        cost_estimate=pl.CostEstimate(
            flops=8 * questions * targets * keys * HEAD,
            bytes_accessed=2 * table.size,
            transcendentals=questions * targets * keys,
        ),
        name="stats",
    )(chosen, query_t, upstream_t, table)


def attend_grads(chosen, query_t, upstream_t, up_weight, stats, table, per_question, slots, span):
    questions, size, targets = query_t.shape
    peers = stats.shape[0]
    one = pl.BlockSpec((1, size, targets), lambda q, c: (q, 0, 0))
    whole = pl.BlockSpec(table.shape, lambda q, c: (0, 0, 0))
    keys = per_question * span
    piece = targets // peers
    in_block = 128 // piece
    latent_shape = (up_weight.shape[0], questions * targets // 128, 128)
    return pl.pallas_call(
        functools.partial(grad_kernel, per_question, slots, span),
        grid_spec=pltpu.PrefetchScalarGridSpec(
            num_scalar_prefetch=1,
            grid=(questions,),
            in_specs=[
                one,
                one,
                pl.BlockSpec(up_weight.shape, lambda q, c: (0, 0)),
                pl.BlockSpec((peers, 1, 8, targets), lambda q, c: (0, q, 0, 0)),
                whole,
            ],
            out_specs=[
                pl.BlockSpec((peers, HEAD, 128), lambda q, c: (0, 0, q // in_block)),
                pl.BlockSpec(latent_shape, lambda q, c: (0, 0, 0)),
                whole,
            ],
        ),
        out_shape=[
            jax.ShapeDtypeStruct((peers, HEAD, questions * piece), F32),
            jax.ShapeDtypeStruct(latent_shape, F32),
            jax.ShapeDtypeStruct(table.shape, BF16),
        ],
        compiler_params=pltpu.CompilerParams(vmem_limit_bytes=VMEM_LIMIT),
        cost_estimate=pl.CostEstimate(
            flops=24 * questions * targets * keys * HEAD,
            bytes_accessed=4 * table.size,
            transcendentals=questions * targets * keys,
        ),
        name="grads",
    )(chosen, query_t, upstream_t, up_weight, stats, table)


def swap_sum(x, axis, shift, radix):
    size = lax.axis_size(axis)
    got = [x] + [
        lax.ppermute(x, axis, [(i, i ^ (k << shift)) for i in range(size)]) for k in range(1, radix)
    ]
    while len(got) > 1:
        got = [a + b for a, b in zip(got[0::2], got[1::2])]
    return got[0]


def to_all(x, axis):
    size = lax.axis_size(axis)
    return lax.all_to_all(
        jnp.broadcast_to(x[None], (size,) + x.shape), axis, split_axis=0, concat_axis=0, tiled=True
    )


def scatter_sum_tp(x):
    size, here = lax.axis_size("tp"), lax.axis_index("tp")
    own = lax.dynamic_index_in_dim(x, here, 0, keepdims=False)
    for k in range(1, size):
        sent = lax.dynamic_index_in_dim(x, (here + k) % size, 0, keepdims=False)
        own = own + lax.ppermute(sent, "tp", [(i, (i + k) % size) for i in range(size)])
    return own


def exchange(x, axis):
    return lax.all_to_all(x, axis, split_axis=0, concat_axis=0, tiled=True)


def local(
    keys,
    values,
    frozen_query_projection,
    context_gradient,
    hidden,
    adapter_down_weight,
    adapter_up_weight,
    owner,
    counts,
    target_length,
):
    group_count, token_split = lax.axis_size("grp"), lax.axis_size("tp")
    questions, targets, _ = frozen_query_projection.shape
    slots_dev, span, _ = keys.shape
    total_slots = group_count * slots_dev
    per_question = (total_slots - group_count // 4) // questions
    piece = targets // token_split
    table_rows = slots_dev * span
    positions = questions * targets
    row_shape = (positions // 128, 128)

    hidden_t = jnp.swapaxes(hidden, 1, 2)
    latent_part = jnp.einsum("dr,qdt->rqt", adapter_down_weight, hidden_t, preferred_element_type=F32)
    live = jnp.arange(slots_dev, dtype=jnp.int32) < counts[0]
    tag = jnp.where(live, owner, questions).astype(F32)
    tags = jnp.broadcast_to(jnp.pad(tag, (0, 128 - slots_dev))[None, None], (group_count, 1, 128))
    sent = jnp.concatenate([latent_part.reshape(group_count, 1, positions), tags], axis=2)
    got = exchange(sent, "grp")
    latent_row = jnp.sum(got[:, 0, :positions], axis=0).astype(BF16).reshape(row_shape)
    slot_key = got[:, 0, positions : positions + slots_dev].astype(jnp.int32).reshape(total_slots)

    packed = pack(keys, values, row_shape[0])
    packed = lax.dynamic_update_slice(
        packed, jnp.broadcast_to(latent_row[None], (group_count,) + row_shape), (0, table_rows, 0)
    )
    table = exchange(packed, "grp")

    slot_ids = jnp.arange(total_slots, dtype=jnp.int32)
    same = (slot_key[:, None] == slot_key[None, :]) & (slot_ids[None, :] < slot_ids[:, None])
    rank = jnp.sum(same.astype(jnp.int32), axis=1)
    place = slot_key * per_question + rank
    wanted = jnp.arange(questions * per_question, dtype=jnp.int32)
    hit = (place[None, :] == wanted[:, None]) & (slot_key < questions)[None, :]
    chosen = jnp.sum(jnp.where(hit, slot_ids[None, :], 0), axis=1)

    step_ids = lax.broadcasted_iota(jnp.int32, (questions, 1, targets), 2)
    keep = step_ids < target_length[:, None, None]
    upstream_t = jnp.swapaxes(context_gradient, 1, 2)
    upstream_t = jnp.where(keep, upstream_t, jnp.zeros_like(upstream_t))
    latent_t = table[:, table_rows:, :].reshape(group_count, questions, targets)
    raised = jnp.einsum("rd,rqt->qdt", adapter_up_weight, latent_t, preferred_element_type=F32)
    frozen_t = jnp.swapaxes(frozen_query_projection, 1, 2)
    query_t = (frozen_t.astype(F32) + raised).astype(BF16)

    stats = attend_stats(chosen, query_t, upstream_t, table, per_question, slots_dev, span)
    dq_parts, latent_grad_part, grad_table = attend_grads(
        chosen,
        query_t,
        upstream_t,
        adapter_up_weight,
        to_all(stats, "tp"),
        table,
        per_question,
        slots_dev,
        span,
    )
    latent_grad_row = jnp.sum(exchange(latent_grad_part, "grp"), axis=0)
    latent_grad_row = jnp.sum(to_all(latent_grad_row, "tp"), axis=0).astype(BF16)
    grad_table = lax.dynamic_update_slice(
        grad_table,
        jnp.broadcast_to(latent_grad_row[None], (group_count,) + row_shape),
        (0, table_rows, 0),
    )
    back = exchange(grad_table, "grp")
    grad_keys, grad_values = unpack(back, slots_dev, span)
    latent_grad = back[:, table_rows:, :].reshape(group_count, questions, targets)
    grad_a = jnp.einsum("qdt,rqt->dr", hidden_t, latent_grad, preferred_element_type=F32)
    grad_a = swap_sum(grad_a, "sect", 0, lax.axis_size("sect"))

    dq_t = scatter_sum_tp(dq_parts).astype(BF16).reshape(HEAD, questions, piece)
    adapted = jnp.transpose(dq_t, (1, 2, 0))
    start = lax.axis_index("tp") * piece
    latent_cut = lax.dynamic_slice_in_dim(latent_t, start, piece, 2)
    grad_b = jnp.einsum("rqt,dqt->rd", latent_cut, dq_t, preferred_element_type=F32)
    grad_b = swap_sum(swap_sum(grad_b, "tp", 0, token_split), "sect", 0, lax.axis_size("sect"))
    return (adapted, grad_keys, grad_values, grad_a, grad_b)


def solution(mesh):
    return jax.shard_map(
        local,
        mesh=mesh,
        in_specs=(
            P(("sect", "grp"), "tp", None),
            P(("sect", "grp"), "tp", None),
            P("sect", None, "grp"),
            P("sect", None, "grp"),
            P("sect", None, "grp"),
            P("grp", None),
            P(None, "grp"),
            P(("sect", "grp")),
            P(("sect", "grp")),
            P("sect"),
        ),
        out_specs=(
            P("sect", "tp", "grp"),
            P(("sect", "grp"), "tp", None),
            P(("sect", "grp"), "tp", None),
            P("grp", None),
            P(None, "grp"),
        ),
        check_vma=False,
    )
```

```python
import functools

import jax
import jax.numpy as jnp
from jax import lax
from jax.experimental import pallas as pl
from jax.experimental.pallas import tpu as pltpu
from jax.sharding import PartitionSpec as P

HEAD = 64
BF16 = jnp.bfloat16
F32 = jnp.float32
VMEM_LIMIT = 32 * 1024 * 1024


def pack_kernel(k_ref, v_ref, o_ref):
    slots, span, width = k_ref.shape
    for pair in range(width // (2 * HEAD)):
        low = pair * 2 * HEAD
        for slot in range(slots):
            rows = pl.ds(slot * span, span)
            k = k_ref[slot, :, low : low + 2 * HEAD]
            v = v_ref[slot, :, low : low + 2 * HEAD]
            o_ref[2 * pair, rows, :] = jnp.concatenate([k[:, :HEAD], v[:, :HEAD]], axis=1)
            o_ref[2 * pair + 1, rows, :] = jnp.concatenate([k[:, HEAD:], v[:, HEAD:]], axis=1)


def unpack_kernel(i_ref, o_ref):
    slots, span, width = o_ref.shape
    for pair in range(width // (2 * HEAD)):
        low = pair * 2 * HEAD
        even = i_ref[2 * pair, :span, :]
        odd = i_ref[2 * pair + 1, :span, :]
        for slot in range(slots):
            side = slice(slot * HEAD, (slot + 1) * HEAD)
            o_ref[slot, :, low : low + 2 * HEAD] = jnp.concatenate([even[:, side], odd[:, side]], axis=1)


PACK_HEADS = 16


def latent_kernel(questions, owner_ref, counts_ref, down_ref, hidden_ref, o_ref):
    down = down_ref[...]
    targets = hidden_ref.shape[2]
    for question in range(questions):
        o_ref[:, 0, question * targets : (question + 1) * targets] = lax.dot_general(
            down, hidden_ref[question], (((0,), (0,)), ((), ())), preferred_element_type=F32
        )
    lanes = lax.broadcasted_iota(jnp.int32, (o_ref.shape[0], 128), 1)
    tags = jnp.zeros(lanes.shape, jnp.int32)
    for slot in range(owner_ref.shape[0]):
        tag = jnp.where(slot < counts_ref[0], owner_ref[slot], questions)
        tags = jnp.where(lanes == slot, tag, tags)
    o_ref[:, 0, questions * targets :] = tags.astype(F32)


def latent_parts(owner, counts, down_weight, hidden_t):
    questions, size, targets = hidden_t.shape
    ranks = down_weight.shape[1]
    smem, vmem = pl.BlockSpec(memory_space=pltpu.SMEM), pl.BlockSpec(memory_space=pltpu.VMEM)
    return pl.pallas_call(
        functools.partial(latent_kernel, questions),
        in_specs=[smem, smem, vmem, vmem],
        out_specs=vmem,
        out_shape=jax.ShapeDtypeStruct((ranks, 1, questions * targets + 128), F32),
        compiler_params=pltpu.CompilerParams(vmem_limit_bytes=VMEM_LIMIT),
        cost_estimate=pl.CostEstimate(
            flops=2 * questions * size * targets * ranks,
            bytes_accessed=6 * questions * size * targets,
            transcendentals=0,
        ),
        name="latent_parts",
    )(owner, counts, down_weight, hidden_t)


def pack(keys, values, spare):
    slots, span, width = keys.shape
    heads, rows = width // HEAD, slots * span + spare
    part = pl.BlockSpec((slots, span, PACK_HEADS * HEAD), lambda i: (0, 0, i))
    return pl.pallas_call(
        pack_kernel,
        grid=(heads // PACK_HEADS,),
        in_specs=[part, part],
        out_specs=pl.BlockSpec((PACK_HEADS, rows, 2 * HEAD), lambda i: (i, 0, 0)),
        out_shape=jax.ShapeDtypeStruct((heads, rows, 2 * HEAD), keys.dtype),
        compiler_params=pltpu.CompilerParams(vmem_limit_bytes=VMEM_LIMIT),
        cost_estimate=pl.CostEstimate(flops=0, bytes_accessed=8 * slots * span * width, transcendentals=0),
        name="pack",
    )(keys, values)


def unpack(table, slots, span):
    heads, rows, _ = table.shape
    return pl.pallas_call(
        unpack_kernel,
        grid=(heads // PACK_HEADS,),
        in_specs=[pl.BlockSpec((PACK_HEADS, rows, 2 * HEAD), lambda i: (i, 0, 0))],
        out_specs=pl.BlockSpec((slots, span, PACK_HEADS * HEAD), lambda i: (0, 0, i)),
        out_shape=jax.ShapeDtypeStruct((slots, span, heads * HEAD), table.dtype),
        compiler_params=pltpu.CompilerParams(vmem_limit_bytes=VMEM_LIMIT),
        cost_estimate=pl.CostEstimate(flops=0, bytes_accessed=4 * slots * span * heads * HEAD, transcendentals=0),
        name="unpack",
    )(table)


STATS_CHUNK = 4
GRAD_CHUNK = 14


def two_sided(q_ref, u_ref):
    q, u = q_ref[0], u_ref[0]
    zero = jnp.zeros_like(q)
    return jnp.concatenate(
        [jnp.concatenate([q, zero], axis=1), jnp.concatenate([zero, u], axis=1)], axis=0
    )


def slot_rows(chosen_ref, slots, span, entry):
    slot = chosen_ref[entry]
    return slot // slots, pl.ds(pl.multiple_of(lax.rem(slot, slots) * span, span), span)


def gathered(chosen_ref, t_ref, slots, span, first, count):
    blocks = []
    for i in range(count):
        device, rows = slot_rows(chosen_ref, slots, span, first + i)
        blocks.append(t_ref[device, rows, :])
    return jnp.concatenate(blocks, axis=0)


def stats_kernel(per_question, slots, span, chosen_ref, q_ref, u_ref, t_ref, o_ref):
    question = pl.program_id(0)
    targets = q_ref.shape[2]
    both = two_sided(q_ref, u_ref)
    top = jnp.full((1, targets), -jnp.inf, F32)
    mass = jnp.zeros((1, targets), F32)
    dot = jnp.zeros((1, targets), F32)
    for chunk in range(per_question // STATS_CHUNK):
        first = question * per_question + chunk * STATS_CHUNK
        rows = gathered(chosen_ref, t_ref, slots, span, first, STATS_CHUNK)
        prod = jnp.dot(rows, both, preferred_element_type=F32)
        scores, prob_grad = prod[:, :targets], prod[:, targets:]
        new_top = jnp.maximum(top, jnp.max(scores, axis=0, keepdims=True))
        scale = jnp.exp(top - new_top)
        exp_scores = jnp.exp(scores - new_top)
        mass = mass * scale + jnp.sum(exp_scores, axis=0, keepdims=True)
        dot = dot * scale + jnp.sum(exp_scores * prob_grad, axis=0, keepdims=True)
        top = new_top
    o_ref[0] = jnp.concatenate([top, mass, dot, jnp.zeros((5, targets), F32)], axis=0)


def row_stats(s_ref):
    members = s_ref.shape[0]
    tops = [s_ref[i, 0, 0:1, :] for i in range(members)]
    top = functools.reduce(jnp.maximum, tops)
    scales = [jnp.exp(t - top) for t in tops]
    inverse = 1.0 / sum(s_ref[i, 0, 1:2, :] * scales[i] for i in range(members))
    delta = sum(s_ref[i, 0, 2:3, :] * scales[i] for i in range(members)) * inverse
    return top, inverse, delta


def chunk_products(chosen_ref, t_ref, slots, span, first, both, stats):
    top, inverse, delta = stats
    targets = top.shape[1]
    rows = gathered(chosen_ref, t_ref, slots, span, first, GRAD_CHUNK)
    prod = jnp.dot(rows, both, preferred_element_type=F32)
    scores, prob_grad = prod[:, :targets], prod[:, targets:]
    weights = jnp.exp(scores - top) * inverse
    score_grad = (weights * (prob_grad - delta)).astype(BF16)
    return rows, weights, score_grad


def store_half(o_ref, slot, slots, value):
    device, span = slot // slots, value.shape[0]
    lanes = lax.broadcasted_iota(jnp.int32, value.shape, 1)
    old = o_ref[device, :span, :]
    o_ref[device, :span, :] = jnp.where(lanes // HEAD == lax.rem(slot, slots), value, old)


def query_value_kernel(
    per_question,
    slots,
    span,
    chosen_ref,
    q_ref,
    u_ref,
    w_ref,
    s_ref,
    t_ref,
    dq_ref,
    o_ref,
    rows_ref,
    grad_ref,
):
    question = pl.program_id(0)
    targets = q_ref.shape[2]
    peers, _, pair_width = dq_ref.shape
    piece = targets // peers

    @pl.when(question == 0)
    def _():
        o_ref[...] = jnp.zeros_like(o_ref)

    both = two_sided(q_ref, u_ref)
    upstream = jnp.concatenate([u_ref[0]] * slots, axis=0)
    stats = row_stats(s_ref)
    size = GRAD_CHUNK * span
    last = (((1,), (1,)), ((), ()))
    for chunk in range(per_question // GRAD_CHUNK):
        first = question * per_question + chunk * GRAD_CHUNK
        rows, weights, score_grad = chunk_products(
            chosen_ref, t_ref, slots, span, first, both, stats
        )
        rows_ref[chunk * size : (chunk + 1) * size, :] = rows
        grad_ref[chunk * size : (chunk + 1) * size, :] = score_grad
        out = lax.dot_general(
            weights.astype(BF16), upstream, last, preferred_element_type=F32
        ).astype(BF16)
        for i in range(GRAD_CHUNK):
            store_half(o_ref, chosen_ref[first + i], slots, out[i * span : (i + 1) * span])
    dq = lax.dot_general(
        rows_ref[...], grad_ref[...], (((0,), (0,)), ((), ())), preferred_element_type=F32
    )[:HEAD]

    for side in range(pair_width // piece):

        @pl.when(question % (pair_width // piece) == side)
        def _():
            for peer in range(peers):
                dq_ref[peer, :, side * piece : (side + 1) * piece] = dq[
                    :, peer * piece : (peer + 1) * piece
                ]

    high = dq.astype(BF16)
    low = (dq - high.astype(F32)).astype(BF16)
    latent = jnp.dot(w_ref[...], high, preferred_element_type=F32) + jnp.dot(
        w_ref[...], low, preferred_element_type=F32
    )
    high = latent.astype(BF16)
    low = (latent - high.astype(F32)).astype(BF16)
    bands = latent.shape[0] // 8
    tiles = o_ref.shape[0] // bands
    for band in range(bands):
        for part in range(targets // 128):
            tile = band * tiles + question * (targets // 128) + part
            cut = (slice(band * 8, (band + 1) * 8), slice(part * 128, (part + 1) * 128))
            o_ref[tile, span : span + 16, :] = jnp.concatenate([high[cut], low[cut]], axis=0)


def key_kernel(per_question, slots, span, chosen_ref, q_ref, u_ref, s_ref, t_ref, o_ref):
    question = pl.program_id(0)

    @pl.when(question == 0)
    def _():
        o_ref[...] = jnp.zeros_like(o_ref)

    both = two_sided(q_ref, u_ref)
    query = jnp.concatenate([q_ref[0]] * slots, axis=0)
    stats = row_stats(s_ref)
    for chunk in range(per_question // GRAD_CHUNK):
        first = question * per_question + chunk * GRAD_CHUNK
        _, _, score_grad = chunk_products(chosen_ref, t_ref, slots, span, first, both, stats)
        out = lax.dot_general(
            score_grad, query, (((1,), (1,)), ((), ())), preferred_element_type=F32
        ).astype(BF16)
        for i in range(GRAD_CHUNK):
            store_half(o_ref, chosen_ref[first + i], slots, out[i * span : (i + 1) * span])


def attend_stats(chosen, query_t, upstream_t, table, per_question, slots, span):
    questions, size, targets = query_t.shape
    one = pl.BlockSpec((1, size, targets), lambda q, c: (q, 0, 0))
    whole = pl.BlockSpec(table.shape, lambda q, c: (0, 0, 0))
    keys = per_question * span
    return pl.pallas_call(
        functools.partial(stats_kernel, per_question, slots, span),
        grid_spec=pltpu.PrefetchScalarGridSpec(
            num_scalar_prefetch=1,
            grid=(questions,),
            in_specs=[one, one, whole],
            out_specs=pl.BlockSpec((1, 8, targets), lambda q, c: (q, 0, 0)),
        ),
        out_shape=jax.ShapeDtypeStruct((questions, 8, targets), F32),
        compiler_params=pltpu.CompilerParams(vmem_limit_bytes=VMEM_LIMIT),
        cost_estimate=pl.CostEstimate(
            flops=8 * questions * targets * keys * HEAD,
            bytes_accessed=2 * table.size,
            transcendentals=questions * targets * keys,
        ),
        name="stats",
    )(chosen, query_t, upstream_t, table)


def query_value_grads(chosen, query_t, upstream_t, up_weight, stats, table, per_question, slots, span):
    questions, size, targets = query_t.shape
    peers = stats.shape[0]
    one = pl.BlockSpec((1, size, targets), lambda q, c: (q, 0, 0))
    whole = pl.BlockSpec(table.shape, lambda q, c: (0, 0, 0))
    out = (table.shape[0], span + 16, table.shape[2])
    keys = per_question * span
    piece = targets // peers
    in_block = 128 // piece
    return pl.pallas_call(
        functools.partial(query_value_kernel, per_question, slots, span),
        grid_spec=pltpu.PrefetchScalarGridSpec(
            num_scalar_prefetch=1,
            grid=(questions,),
            in_specs=[
                one,
                one,
                pl.BlockSpec(up_weight.shape, lambda q, c: (0, 0)),
                pl.BlockSpec((peers, 1, 8, targets), lambda q, c: (0, q, 0, 0)),
                whole,
            ],
            out_specs=[
                pl.BlockSpec((peers, size, 128), lambda q, c: (0, 0, q // in_block)),
                pl.BlockSpec(out, lambda q, c: (0, 0, 0)),
            ],
            scratch_shapes=[pltpu.VMEM((keys, 2 * HEAD), BF16), pltpu.VMEM((keys, targets), BF16)],
        ),
        out_shape=[
            jax.ShapeDtypeStruct((peers, size, questions * piece), F32),
            jax.ShapeDtypeStruct(out, BF16),
        ],
        compiler_params=pltpu.CompilerParams(vmem_limit_bytes=VMEM_LIMIT),
        cost_estimate=pl.CostEstimate(
            flops=24 * questions * targets * keys * HEAD,
            bytes_accessed=4 * table.size,
            transcendentals=questions * targets * keys,
        ),
        name="query_value_grads",
    )(chosen, query_t, upstream_t, up_weight, stats, table)


def key_grads(chosen, query_t, upstream_t, stats, table, per_question, slots, span):
    questions, size, targets = query_t.shape
    peers = stats.shape[0]
    one = pl.BlockSpec((1, size, targets), lambda q, c: (q, 0, 0))
    whole = pl.BlockSpec(table.shape, lambda q, c: (0, 0, 0))
    out = (table.shape[0], span + 8, table.shape[2])
    keys = per_question * span
    return pl.pallas_call(
        functools.partial(key_kernel, per_question, slots, span),
        grid_spec=pltpu.PrefetchScalarGridSpec(
            num_scalar_prefetch=1,
            grid=(questions,),
            in_specs=[
                one,
                one,
                pl.BlockSpec((peers, 1, 8, targets), lambda q, c: (0, q, 0, 0)),
                whole,
            ],
            out_specs=pl.BlockSpec(out, lambda q, c: (0, 0, 0)),
        ),
        out_shape=jax.ShapeDtypeStruct(out, BF16),
        compiler_params=pltpu.CompilerParams(vmem_limit_bytes=VMEM_LIMIT),
        cost_estimate=pl.CostEstimate(
            flops=16 * questions * targets * keys * HEAD,
            bytes_accessed=4 * table.size,
            transcendentals=questions * targets * keys,
        ),
        name="key_grads",
    )(chosen, query_t, upstream_t, stats, table)


def to_all(x, axis):
    size = lax.axis_size(axis)
    return exchange(
        jnp.broadcast_to(x[None], (size,) + x.shape), axis
    )


def scatter_sum_tp(x):
    size, here = lax.axis_size("tp"), lax.axis_index("tp")
    own = lax.dynamic_index_in_dim(x, here, 0, keepdims=False)
    for k in range(1, size):
        sent = lax.dynamic_index_in_dim(x, (here + k) % size, 0, keepdims=False)
        own = own + lax.ppermute(sent, "tp", [(i, (i + k) % size) for i in range(size)])
    return own


def exchange(x, axis):
    return lax.all_to_all(x, axis, split_axis=0, concat_axis=0, tiled=True)


def local(
    keys,
    values,
    frozen_query_projection,
    context_gradient,
    hidden,
    adapter_down_weight,
    adapter_up_weight,
    owner,
    counts,
    target_length,
):
    group_count, token_split = lax.axis_size("grp"), lax.axis_size("tp")
    questions, targets, _ = frozen_query_projection.shape
    slots_dev, span, _ = keys.shape
    total_slots = group_count * slots_dev
    per_question = (total_slots - group_count // 4) // questions
    piece = targets // token_split
    table_rows = slots_dev * span
    positions = questions * targets
    row_shape = (positions // 128, 128)

    hidden_t = jnp.swapaxes(hidden, 1, 2)
    sent = latent_parts(owner, counts, adapter_down_weight, hidden_t)
    got = exchange(sent, "grp")
    latent_row = jnp.sum(got[:, 0, :positions], axis=0).astype(BF16).reshape(row_shape)
    slot_key = got[:, 0, positions : positions + slots_dev].astype(jnp.int32).reshape(total_slots)

    packed = pack(keys, values, row_shape[0])
    packed = lax.dynamic_update_slice(
        packed, jnp.broadcast_to(latent_row[None], (group_count,) + row_shape), (0, table_rows, 0)
    )
    table = exchange(packed, "grp")

    slot_ids = jnp.arange(total_slots, dtype=jnp.int32)
    same = (slot_key[:, None] == slot_key[None, :]) & (slot_ids[None, :] < slot_ids[:, None])
    rank = jnp.sum(same.astype(jnp.int32), axis=1)
    place = slot_key * per_question + rank
    wanted = jnp.arange(questions * per_question, dtype=jnp.int32)
    hit = (place[None, :] == wanted[:, None]) & (slot_key < questions)[None, :]
    chosen = jnp.sum(jnp.where(hit, slot_ids[None, :], 0), axis=1)

    step_ids = lax.broadcasted_iota(jnp.int32, (questions, 1, targets), 2)
    keep = step_ids < target_length[:, None, None]
    upstream_t = jnp.swapaxes(context_gradient, 1, 2)
    upstream_t = jnp.where(keep, upstream_t, jnp.zeros_like(upstream_t))
    latent_t = table[:, table_rows:, :].reshape(group_count, questions, targets)
    raised = jnp.einsum("rd,rqt->qdt", adapter_up_weight, latent_t, preferred_element_type=F32)
    frozen_t = jnp.swapaxes(frozen_query_projection, 1, 2)
    query_t = (frozen_t.astype(F32) + raised).astype(BF16)

    stats = attend_stats(chosen, query_t, upstream_t, table, per_question, slots_dev, span)
    all_stats = to_all(stats, "tp")
    shared = (table, per_question, slots_dev, span)
    dq_parts, value_table = query_value_grads(
        chosen, query_t, upstream_t, adapter_up_weight, all_stats, *shared
    )
    key_table = key_grads(chosen, query_t, upstream_t, all_stats, *shared)
    value_back = exchange(value_table, "grp")
    latent_grad_tile = jnp.sum(value_back[:, span:, :].astype(F32), axis=0)
    latent_grad_tile = (latent_grad_tile[:8] + latent_grad_tile[8:]).astype(BF16)
    key_table = lax.dynamic_update_slice(
        key_table,
        jnp.broadcast_to(latent_grad_tile[None], (group_count,) + latent_grad_tile.shape),
        (0, span, 0),
    )
    grad_values = unpack(value_back, slots_dev, span)
    key_back = exchange(key_table, "grp")
    grad_keys = unpack(key_back, slots_dev, span)
    latent_grad = key_back[:, span:, :].reshape(HEAD // 8, positions // 128, 8, 128)
    latent_grad = jnp.transpose(latent_grad, (0, 2, 1, 3)).reshape(HEAD, questions, targets)
    grad_a = jnp.einsum("qdt,rqt->dr", hidden_t, latent_grad, preferred_element_type=F32)

    dq_t = scatter_sum_tp(dq_parts).astype(BF16).reshape(HEAD, questions, piece)
    adapted = jnp.transpose(dq_t, (1, 2, 0))
    start = lax.axis_index("tp") * piece
    latent_cut = lax.dynamic_slice_in_dim(latent_t, start, piece, 2)
    grad_b = jnp.einsum("rqt,dqt->rd", latent_cut, dq_t, preferred_element_type=F32)
    got = to_all(jnp.concatenate([grad_a, grad_b], axis=1), ("sect", "tp"))
    got, grad_keys = lax.optimization_barrier((got, grad_keys))
    grads = jnp.sum(got, axis=0)
    return (adapted, grad_keys, grad_values, grads[:, :HEAD], grads[:, HEAD:])


def solution(mesh):
    return jax.shard_map(
        local,
        mesh=mesh,
        in_specs=(
            P(("sect", "grp"), "tp", None),
            P(("sect", "grp"), "tp", None),
            P("sect", None, "grp"),
            P("sect", None, "grp"),
            P("sect", None, "grp"),
            P("grp", None),
            P(None, "grp"),
            P(("sect", "grp")),
            P(("sect", "grp")),
            P("sect"),
        ),
        out_specs=(
            P("sect", "tp", "grp"),
            P(("sect", "grp"), "tp", None),
            P(("sect", "grp"), "tp", None),
            P("grp", None),
            P(None, "grp"),
        ),
        check_vma=False,
    )
```

```python
import functools

import jax
import jax.numpy as jnp
from jax import lax
from jax.experimental import pallas as pl
from jax.experimental.pallas import tpu as pltpu
from jax.sharding import PartitionSpec as P

HEAD = 64
BF16 = jnp.bfloat16
F32 = jnp.float32
VMEM_LIMIT = 32 * 1024 * 1024
ALL_VMEM = 62 * 1024 * 1024


def reverse(index, size):
    bits = size.bit_length() - 1
    return sum(((index >> bit) & 1) << (bits - 1 - bit) for bit in range(bits))


def pack_kernel(k_ref, v_ref, o_ref):
    slots, span, width = k_ref.shape
    heads = width // HEAD
    for pair in range(width // (2 * HEAD)):
        low = pair * 2 * HEAD
        for slot in range(slots):
            rows = pl.ds(slot * span, span)
            k = k_ref[slot, :, low : low + 2 * HEAD]
            v = v_ref[slot, :, low : low + 2 * HEAD]
            o_ref[reverse(2 * pair, heads), 0, rows, :] = jnp.concatenate([k[:, :HEAD], v[:, :HEAD]], axis=1)
            o_ref[reverse(2 * pair + 1, heads), 0, rows, :] = jnp.concatenate([k[:, HEAD:], v[:, HEAD:]], axis=1)


def unpack_kernel(i_ref, o_ref):
    slots, span, width = o_ref.shape
    heads = width // HEAD
    for pair in range(width // (2 * HEAD)):
        low = pair * 2 * HEAD
        even = i_ref[reverse(2 * pair, heads), 0, :span, :]
        odd = i_ref[reverse(2 * pair + 1, heads), 0, :span, :]
        for slot in range(slots):
            side = slice(slot * HEAD, (slot + 1) * HEAD)
            o_ref[slot, :, low : low + 2 * HEAD] = jnp.concatenate([even[:, side], odd[:, side]], axis=1)


PACK_HEADS = 16


def latent_kernel(questions, owner_ref, counts_ref, down_ref, hidden_ref, o_ref):
    down = down_ref[...]
    targets = hidden_ref.shape[2]
    for question in range(questions):
        o_ref[:, 0, question * targets : (question + 1) * targets] = lax.dot_general(
            down, hidden_ref[question], (((0,), (0,)), ((), ())), preferred_element_type=F32
        )
    lanes = lax.broadcasted_iota(jnp.int32, (o_ref.shape[0], 128), 1)
    tags = jnp.zeros(lanes.shape, jnp.int32)
    for slot in range(owner_ref.shape[0]):
        tag = jnp.where(slot < counts_ref[0], owner_ref[slot], questions)
        tags = jnp.where(lanes == slot, tag, tags)
    o_ref[:, 0, questions * targets :] = tags.astype(F32)


def latent_parts(owner, counts, down_weight, hidden_t):
    questions, size, targets = hidden_t.shape
    ranks = down_weight.shape[1]
    smem, vmem = pl.BlockSpec(memory_space=pltpu.SMEM), pl.BlockSpec(memory_space=pltpu.VMEM)
    return pl.pallas_call(
        functools.partial(latent_kernel, questions),
        in_specs=[smem, smem, vmem, vmem],
        out_specs=vmem,
        out_shape=jax.ShapeDtypeStruct((ranks, 1, questions * targets + 128), F32),
        compiler_params=pltpu.CompilerParams(vmem_limit_bytes=ALL_VMEM),
        cost_estimate=pl.CostEstimate(
            flops=2 * questions * size * targets * ranks,
            bytes_accessed=6 * questions * size * targets,
            transcendentals=0,
        ),
        name="latent_parts",
    )(owner, counts, down_weight, hidden_t)


def pack(keys, values, spare):
    slots, span, width = keys.shape
    heads, rows = width // HEAD, slots * span + spare
    steps = heads // PACK_HEADS
    part = pl.BlockSpec((slots, span, PACK_HEADS * HEAD), lambda i: (0, 0, i))
    return pl.pallas_call(
        pack_kernel,
        grid=(steps,),
        in_specs=[part, part],
        out_specs=pl.BlockSpec(
            (PACK_HEADS, 1, rows, 2 * HEAD), lambda i: (0, reverse(i, steps), 0, 0)
        ),
        out_shape=jax.ShapeDtypeStruct((PACK_HEADS, steps, rows, 2 * HEAD), keys.dtype),
        compiler_params=pltpu.CompilerParams(vmem_limit_bytes=VMEM_LIMIT),
        cost_estimate=pl.CostEstimate(flops=0, bytes_accessed=8 * slots * span * width, transcendentals=0),
        name="pack",
    )(keys, values).reshape(heads, rows, 2 * HEAD)


def unpack(table, slots, span):
    heads, rows, _ = table.shape
    steps = heads // PACK_HEADS
    return pl.pallas_call(
        unpack_kernel,
        grid=(steps,),
        in_specs=[
            pl.BlockSpec((PACK_HEADS, 1, rows, 2 * HEAD), lambda i: (0, reverse(i, steps), 0, 0))
        ],
        out_specs=pl.BlockSpec((slots, span, PACK_HEADS * HEAD), lambda i: (0, 0, i)),
        out_shape=jax.ShapeDtypeStruct((slots, span, heads * HEAD), table.dtype),
        compiler_params=pltpu.CompilerParams(vmem_limit_bytes=VMEM_LIMIT),
        cost_estimate=pl.CostEstimate(flops=0, bytes_accessed=4 * slots * span * heads * HEAD, transcendentals=0),
        name="unpack",
    )(table.reshape(PACK_HEADS, steps, rows, 2 * HEAD))


STATS_CHUNK = 4
GRAD_CHUNK = 14


def two_sided(q_ref, u_ref):
    q, u = q_ref[0], u_ref[0]
    zero = jnp.zeros_like(q)
    return jnp.concatenate(
        [jnp.concatenate([q, zero], axis=1), jnp.concatenate([zero, u], axis=1)], axis=0
    )


def slot_rows(chosen_ref, slots, span, entry):
    slot = chosen_ref[entry]
    return slot // slots, pl.ds(pl.multiple_of(lax.rem(slot, slots) * span, span), span)


def gathered(chosen_ref, t_ref, slots, span, first, count):
    blocks = []
    for i in range(count):
        device, rows = slot_rows(chosen_ref, slots, span, first + i)
        blocks.append(t_ref[device, rows, :])
    return jnp.concatenate(blocks, axis=0)


def stats_kernel(per_question, slots, span, chosen_ref, q_ref, u_ref, t_ref, o_ref):
    question = pl.program_id(0)
    targets = q_ref.shape[2]
    both = two_sided(q_ref, u_ref)
    top = jnp.full((1, targets), -jnp.inf, F32)
    mass = jnp.zeros((1, targets), F32)
    dot = jnp.zeros((1, targets), F32)
    for chunk in range(per_question // STATS_CHUNK):
        first = question * per_question + chunk * STATS_CHUNK
        rows = gathered(chosen_ref, t_ref, slots, span, first, STATS_CHUNK)
        prod = jnp.dot(rows, both, preferred_element_type=F32)
        scores, prob_grad = prod[:, :targets], prod[:, targets:]
        new_top = jnp.maximum(top, jnp.max(scores, axis=0, keepdims=True))
        scale = jnp.exp(top - new_top)
        exp_scores = jnp.exp(scores - new_top)
        mass = mass * scale + jnp.sum(exp_scores, axis=0, keepdims=True)
        dot = dot * scale + jnp.sum(exp_scores * prob_grad, axis=0, keepdims=True)
        top = new_top
    o_ref[0] = jnp.concatenate([top, mass, dot, jnp.zeros((5, targets), F32)], axis=0)


def row_stats(s_ref):
    members = s_ref.shape[0]
    tops = [s_ref[i, 0, 0:1, :] for i in range(members)]
    top = functools.reduce(jnp.maximum, tops)
    scales = [jnp.exp(t - top) for t in tops]
    inverse = 1.0 / sum(s_ref[i, 0, 1:2, :] * scales[i] for i in range(members))
    delta = sum(s_ref[i, 0, 2:3, :] * scales[i] for i in range(members)) * inverse
    return top, inverse, delta


def chunk_products(chosen_ref, t_ref, slots, span, first, both, stats):
    top, inverse, delta = stats
    targets = top.shape[1]
    rows = gathered(chosen_ref, t_ref, slots, span, first, GRAD_CHUNK)
    prod = jnp.dot(rows, both, preferred_element_type=F32)
    scores, prob_grad = prod[:, :targets], prod[:, targets:]
    weights = jnp.exp(scores - top) * inverse
    score_grad = (weights * (prob_grad - delta)).astype(BF16)
    return rows, weights, score_grad


def store_half(o_ref, slot, slots, value):
    device, span = slot // slots, value.shape[0]
    lanes = lax.broadcasted_iota(jnp.int32, value.shape, 1)
    old = o_ref[device, :span, :]
    o_ref[device, :span, :] = jnp.where(lanes // HEAD == lax.rem(slot, slots), value, old)


def query_value_kernel(
    per_question,
    slots,
    span,
    chosen_ref,
    q_ref,
    u_ref,
    w_ref,
    s_ref,
    t_ref,
    dq_ref,
    o_ref,
    rows_ref,
    grad_ref,
):
    question = pl.program_id(0)
    targets = q_ref.shape[2]
    peers, _, pair_width = dq_ref.shape
    piece = targets // peers

    @pl.when(question == 0)
    def _():
        o_ref[...] = jnp.zeros_like(o_ref)

    both = two_sided(q_ref, u_ref)
    upstream = jnp.concatenate([u_ref[0]] * slots, axis=0)
    stats = row_stats(s_ref)
    size = GRAD_CHUNK * span
    last = (((1,), (1,)), ((), ()))
    for chunk in range(per_question // GRAD_CHUNK):
        first = question * per_question + chunk * GRAD_CHUNK
        rows, weights, score_grad = chunk_products(
            chosen_ref, t_ref, slots, span, first, both, stats
        )
        rows_ref[chunk * size : (chunk + 1) * size, :] = rows
        grad_ref[chunk * size : (chunk + 1) * size, :] = score_grad
        out = lax.dot_general(
            weights.astype(BF16), upstream, last, preferred_element_type=F32
        ).astype(BF16)
        for i in range(GRAD_CHUNK):
            store_half(o_ref, chosen_ref[first + i], slots, out[i * span : (i + 1) * span])
    dq = lax.dot_general(
        rows_ref[...], grad_ref[...], (((0,), (0,)), ((), ())), preferred_element_type=F32
    )[:HEAD]

    for side in range(pair_width // piece):

        @pl.when(question % (pair_width // piece) == side)
        def _():
            for peer in range(peers):
                dq_ref[peer, :, side * piece : (side + 1) * piece] = dq[
                    :, peer * piece : (peer + 1) * piece
                ]

    high = dq.astype(BF16)
    low = (dq - high.astype(F32)).astype(BF16)
    latent = jnp.dot(w_ref[...], high, preferred_element_type=F32) + jnp.dot(
        w_ref[...], low, preferred_element_type=F32
    )
    high = latent.astype(BF16)
    low = (latent - high.astype(F32)).astype(BF16)
    bands = latent.shape[0] // 8
    tiles = o_ref.shape[0] // bands
    for band in range(bands):
        for part in range(targets // 128):
            tile = band * tiles + question * (targets // 128) + part
            cut = (slice(band * 8, (band + 1) * 8), slice(part * 128, (part + 1) * 128))
            o_ref[tile, span : span + 16, :] = jnp.concatenate([high[cut], low[cut]], axis=0)


def key_kernel(per_question, slots, span, chosen_ref, q_ref, u_ref, s_ref, t_ref, o_ref):
    question = pl.program_id(0)

    @pl.when(question == 0)
    def _():
        o_ref[...] = jnp.zeros_like(o_ref)

    both = two_sided(q_ref, u_ref)
    query = jnp.concatenate([q_ref[0]] * slots, axis=0)
    stats = row_stats(s_ref)
    for chunk in range(per_question // GRAD_CHUNK):
        first = question * per_question + chunk * GRAD_CHUNK
        _, _, score_grad = chunk_products(chosen_ref, t_ref, slots, span, first, both, stats)
        out = lax.dot_general(
            score_grad, query, (((1,), (1,)), ((), ())), preferred_element_type=F32
        ).astype(BF16)
        for i in range(GRAD_CHUNK):
            store_half(o_ref, chosen_ref[first + i], slots, out[i * span : (i + 1) * span])


def attend_stats(chosen, query_t, upstream_t, table, per_question, slots, span):
    questions, size, targets = query_t.shape
    one = pl.BlockSpec((1, size, targets), lambda q, c: (q, 0, 0))
    whole = pl.BlockSpec(table.shape, lambda q, c: (0, 0, 0))
    keys = per_question * span
    return pl.pallas_call(
        functools.partial(stats_kernel, per_question, slots, span),
        grid_spec=pltpu.PrefetchScalarGridSpec(
            num_scalar_prefetch=1,
            grid=(questions,),
            in_specs=[one, one, whole],
            out_specs=pl.BlockSpec((1, 8, targets), lambda q, c: (q, 0, 0)),
        ),
        out_shape=jax.ShapeDtypeStruct((questions, 8, targets), F32),
        compiler_params=pltpu.CompilerParams(vmem_limit_bytes=VMEM_LIMIT),
        cost_estimate=pl.CostEstimate(
            flops=8 * questions * targets * keys * HEAD,
            bytes_accessed=2 * table.size,
            transcendentals=questions * targets * keys,
        ),
        name="stats",
    )(chosen, query_t, upstream_t, table)


def query_value_grads(chosen, query_t, upstream_t, up_weight, stats, table, per_question, slots, span):
    questions, size, targets = query_t.shape
    peers = stats.shape[0]
    one = pl.BlockSpec((1, size, targets), lambda q, c: (q, 0, 0))
    whole = pl.BlockSpec(table.shape, lambda q, c: (0, 0, 0))
    out = (table.shape[0], span + 16, table.shape[2])
    keys = per_question * span
    piece = targets // peers
    in_block = 128 // piece
    return pl.pallas_call(
        functools.partial(query_value_kernel, per_question, slots, span),
        grid_spec=pltpu.PrefetchScalarGridSpec(
            num_scalar_prefetch=1,
            grid=(questions,),
            in_specs=[
                one,
                one,
                pl.BlockSpec(up_weight.shape, lambda q, c: (0, 0)),
                pl.BlockSpec((peers, 1, 8, targets), lambda q, c: (0, q, 0, 0)),
                whole,
            ],
            out_specs=[
                pl.BlockSpec((peers, size, 128), lambda q, c: (0, 0, q // in_block)),
                pl.BlockSpec(out, lambda q, c: (0, 0, 0)),
            ],
            scratch_shapes=[pltpu.VMEM((keys, 2 * HEAD), BF16), pltpu.VMEM((keys, targets), BF16)],
        ),
        out_shape=[
            pltpu.HBM((peers, size, questions * piece), F32),
            pltpu.HBM(out, BF16),
        ],
        compiler_params=pltpu.CompilerParams(vmem_limit_bytes=VMEM_LIMIT),
        cost_estimate=pl.CostEstimate(
            flops=24 * questions * targets * keys * HEAD,
            bytes_accessed=4 * table.size,
            transcendentals=questions * targets * keys,
        ),
        name="query_value_grads",
    )(chosen, query_t, upstream_t, up_weight, stats, table)


def key_grads(chosen, query_t, upstream_t, stats, table, per_question, slots, span):
    questions, size, targets = query_t.shape
    peers = stats.shape[0]
    one = pl.BlockSpec((1, size, targets), lambda q, c: (q, 0, 0))
    whole = pl.BlockSpec(table.shape, lambda q, c: (0, 0, 0))
    out = (table.shape[0], span + 8, table.shape[2])
    keys = per_question * span
    return pl.pallas_call(
        functools.partial(key_kernel, per_question, slots, span),
        grid_spec=pltpu.PrefetchScalarGridSpec(
            num_scalar_prefetch=1,
            grid=(questions,),
            in_specs=[
                one,
                one,
                pl.BlockSpec((peers, 1, 8, targets), lambda q, c: (0, q, 0, 0)),
                whole,
            ],
            out_specs=pl.BlockSpec(out, lambda q, c: (0, 0, 0)),
        ),
        out_shape=pltpu.HBM(out, BF16),
        compiler_params=pltpu.CompilerParams(vmem_limit_bytes=VMEM_LIMIT),
        cost_estimate=pl.CostEstimate(
            flops=16 * questions * targets * keys * HEAD,
            bytes_accessed=4 * table.size,
            transcendentals=questions * targets * keys,
        ),
        name="key_grads",
    )(chosen, query_t, upstream_t, stats, table)


def to_all(x, axis):
    size = lax.axis_size(axis)
    return exchange(
        jnp.broadcast_to(x[None], (size,) + x.shape), axis
    )


def scatter_sum_tp(x):
    size, here = lax.axis_size("tp"), lax.axis_index("tp")
    own = lax.dynamic_index_in_dim(x, here, 0, keepdims=False)
    for k in range(1, size):
        sent = lax.dynamic_index_in_dim(x, (here + k) % size, 0, keepdims=False)
        own = own + lax.ppermute(sent, "tp", [(i, (i + k) % size) for i in range(size)])
    return own


def exchange(x, axis):
    order = None
    if axis == "grp":
        size = lax.axis_size(axis)
        order = [[reverse(i, size) for i in range(size)]]
    return lax.all_to_all(
        x, axis, split_axis=0, concat_axis=0, tiled=True, axis_index_groups=order
    )


def local(
    keys,
    values,
    frozen_query_projection,
    context_gradient,
    hidden,
    adapter_down_weight,
    adapter_up_weight,
    owner,
    counts,
    target_length,
):
    group_count, token_split = lax.axis_size("grp"), lax.axis_size("tp")
    questions, targets, _ = frozen_query_projection.shape
    slots_dev, span, _ = keys.shape
    total_slots = group_count * slots_dev
    per_question = (total_slots - group_count // 4) // questions
    piece = targets // token_split
    table_rows = slots_dev * span
    positions = questions * targets
    row_shape = (positions // 128, 128)

    hidden_t = jnp.swapaxes(hidden, 1, 2)
    sent = latent_parts(owner, counts, adapter_down_weight, hidden_t)
    got = exchange(sent, "grp")
    latent_row = jnp.sum(got[:, 0, :positions], axis=0).astype(BF16).reshape(row_shape)
    slot_key = got[:, 0, positions : positions + slots_dev].astype(jnp.int32).reshape(total_slots)

    packed = pack(keys, values, row_shape[0])
    packed = lax.dynamic_update_slice(
        packed, jnp.broadcast_to(latent_row[None], (group_count,) + row_shape), (0, table_rows, 0)
    )
    table = exchange(packed, "grp")

    slot_ids = jnp.arange(total_slots, dtype=jnp.int32)
    same = (slot_key[:, None] == slot_key[None, :]) & (slot_ids[None, :] < slot_ids[:, None])
    rank = jnp.sum(same.astype(jnp.int32), axis=1)
    place = slot_key * per_question + rank
    wanted = jnp.arange(questions * per_question, dtype=jnp.int32)
    hit = (place[None, :] == wanted[:, None]) & (slot_key < questions)[None, :]
    chosen = jnp.sum(jnp.where(hit, slot_ids[None, :], 0), axis=1)

    step_ids = lax.broadcasted_iota(jnp.int32, (questions, 1, targets), 2)
    keep = step_ids < target_length[:, None, None]
    upstream_t = jnp.swapaxes(context_gradient, 1, 2)
    upstream_t = jnp.where(keep, upstream_t, jnp.zeros_like(upstream_t))
    latent_t = table[:, table_rows:, :].reshape(group_count, questions, targets)
    raised = jnp.einsum("rd,rqt->qdt", adapter_up_weight, latent_t, preferred_element_type=F32)
    frozen_t = jnp.swapaxes(frozen_query_projection, 1, 2)
    query_t = (frozen_t.astype(F32) + raised).astype(BF16)

    stats = attend_stats(chosen, query_t, upstream_t, table, per_question, slots_dev, span)
    all_stats = to_all(stats, "tp")
    shared = (table, per_question, slots_dev, span)
    dq_parts, value_table = query_value_grads(
        chosen, query_t, upstream_t, adapter_up_weight, all_stats, *shared
    )
    key_table = key_grads(chosen, query_t, upstream_t, all_stats, *shared)
    value_back = exchange(value_table, "grp")
    latent_grad_tile = jnp.sum(value_back[:, span:, :].astype(F32), axis=0)
    latent_grad_tile = (latent_grad_tile[:8] + latent_grad_tile[8:]).astype(BF16)
    key_table = lax.dynamic_update_slice(
        key_table,
        jnp.broadcast_to(latent_grad_tile[None], (group_count,) + latent_grad_tile.shape),
        (0, span, 0),
    )
    grad_values = unpack(value_back, slots_dev, span)
    key_back = exchange(key_table, "grp")
    grad_keys = unpack(key_back, slots_dev, span)
    latent_grad = key_back[:, span:, :].reshape(HEAD // 8, positions // 128, 8, 128)
    latent_grad = jnp.transpose(latent_grad, (0, 2, 1, 3)).reshape(HEAD, questions, targets)
    grad_a = jnp.einsum("qdt,rqt->dr", hidden_t, latent_grad, preferred_element_type=F32)

    dq_t = scatter_sum_tp(dq_parts).astype(BF16).reshape(HEAD, questions, piece)
    adapted = jnp.transpose(dq_t, (1, 2, 0))
    start = lax.axis_index("tp") * piece
    latent_cut = lax.dynamic_slice_in_dim(latent_t, start, piece, 2)
    grad_b = jnp.einsum("rqt,dqt->rd", latent_cut, dq_t, preferred_element_type=F32)
    got = to_all(jnp.concatenate([grad_a, grad_b], axis=1), ("sect", "tp"))
    got, grad_keys = lax.optimization_barrier((got, grad_keys))
    grads = jnp.sum(got, axis=0)
    return (adapted, grad_keys, grad_values, grads[:, :HEAD], grads[:, HEAD:])


def solution(mesh):
    return jax.shard_map(
        local,
        mesh=mesh,
        in_specs=(
            P(("sect", "grp"), "tp", None),
            P(("sect", "grp"), "tp", None),
            P("sect", None, "grp"),
            P("sect", None, "grp"),
            P("sect", None, "grp"),
            P("grp", None),
            P(None, "grp"),
            P(("sect", "grp")),
            P(("sect", "grp")),
            P("sect"),
        ),
        out_specs=(
            P("sect", "tp", "grp"),
            P(("sect", "grp"), "tp", None),
            P(("sect", "grp"), "tp", None),
            P("grp", None),
            P(None, "grp"),
        ),
        check_vma=False,
    )
```

```python
import functools

import jax
import jax.numpy as jnp
from jax import lax
from jax.experimental import pallas as pl
from jax.experimental.pallas import tpu as pltpu
from jax.sharding import PartitionSpec as P

HEAD = 64
BF16 = jnp.bfloat16
F32 = jnp.float32
VMEM_LIMIT = 32 * 1024 * 1024
ALL_VMEM = 62 * 1024 * 1024


def reverse(index, size):
    bits = size.bit_length() - 1
    return sum(((index >> bit) & 1) << (bits - 1 - bit) for bit in range(bits))


def pack_rows(x_ref, o_ref):
    slots, span, width = x_ref.shape
    heads = width // HEAD
    for pair in range(width // (2 * HEAD)):
        low = pair * 2 * HEAD
        parts = [x_ref[slot, :, low : low + 2 * HEAD] for slot in range(slots)]
        for side in range(2):
            cut = slice(side * HEAD, (side + 1) * HEAD)
            o_ref[reverse(2 * pair + side, heads), 0, :span, :] = jnp.concatenate(
                [part[:, cut] for part in parts], axis=1
            )


def pack_key_kernel(k_ref, o_ref):
    pack_rows(k_ref, o_ref)


def pack_value_kernel(owner_ref, counts_ref, down_ref, hidden_ref, v_ref, o_ref):
    pack_rows(v_ref, o_ref)
    span = v_ref.shape[1]
    questions, _, targets = hidden_ref.shape
    blocks, steps = o_ref.shape[0], pl.num_programs(0)
    halves = targets // 128
    lanes = lax.broadcasted_iota(jnp.int32, (8, 128), 1)
    tags = jnp.zeros(lanes.shape, jnp.int32)
    for slot in range(owner_ref.shape[0]):
        tag = jnp.where(slot < counts_ref[0], owner_ref[slot], questions)
        tags = jnp.where(lanes == slot, tag, tags)
    tags = tags.astype(F32)
    down = down_ref[...]
    bands = down.shape[1] // 8
    per_band = blocks // bands
    step = reverse(pl.program_id(0), PACK_STEPS)
    for turn in range(per_band):
        part = turn * steps + step
        start = pl.multiple_of(lax.rem(part, halves) * 128, 128)
        latent = lax.dot_general(
            down,
            hidden_ref[part // halves, :, pl.ds(start, 128)],
            (((0,), (0,)), ((), ())),
            preferred_element_type=F32,
        )
        for band in range(bands):
            tile = latent[band * 8 : (band + 1) * 8]
            o_ref[band * per_band + turn, 0, span : span + 16, :] = jnp.concatenate(
                [tile, tags], axis=0
            ).astype(o_ref.dtype)


def unpack_kernel(i_ref, o_ref):
    slots, span, width = o_ref.shape
    heads = width // HEAD
    for pair in range(width // (2 * HEAD)):
        low = pair * 2 * HEAD
        even = i_ref[reverse(2 * pair, heads), 0, :span, :]
        odd = i_ref[reverse(2 * pair + 1, heads), 0, :span, :]
        for slot in range(slots):
            side = slice(slot * HEAD, (slot + 1) * HEAD)
            o_ref[slot, :, low : low + 2 * HEAD] = jnp.concatenate([even[:, side], odd[:, side]], axis=1)


PACK_STEPS = 4


def pack_specs(slots, span, width, rows):
    heads = width // HEAD
    blocks = heads // PACK_STEPS
    part = pl.BlockSpec((slots, span, blocks * HEAD), lambda i: (0, 0, i))
    table = pl.BlockSpec(
        (blocks, 1, rows, slots * HEAD), lambda i: (0, reverse(i, PACK_STEPS), 0, 0)
    )
    return part, table, (blocks, PACK_STEPS, rows, slots * HEAD)


def pack_keys(keys, spare):
    slots, span, width = keys.shape
    part, table, shape = pack_specs(slots, span, width, span + spare)
    packed = pl.pallas_call(
        pack_key_kernel,
        grid=(PACK_STEPS,),
        in_specs=[part],
        out_specs=table,
        out_shape=jax.ShapeDtypeStruct(shape, keys.dtype),
        compiler_params=pltpu.CompilerParams(vmem_limit_bytes=VMEM_LIMIT),
        cost_estimate=pl.CostEstimate(flops=0, bytes_accessed=4 * keys.size, transcendentals=0),
        name="pack_keys",
    )(keys)
    return packed.reshape(width // HEAD, span + spare, slots * HEAD)


def pack_values(owner, counts, down_weight, hidden_t, values):
    slots, span, width = values.shape
    part, table, shape = pack_specs(slots, span, width, span + 16)
    smem = pl.BlockSpec(memory_space=pltpu.SMEM)
    packed = pl.pallas_call(
        pack_value_kernel,
        grid=(PACK_STEPS,),
        in_specs=[
            smem,
            smem,
            pl.BlockSpec(down_weight.shape, lambda i: (0, 0)),
            pl.BlockSpec(hidden_t.shape, lambda i: (0, 0, 0)),
            part,
        ],
        out_specs=table,
        out_shape=jax.ShapeDtypeStruct(shape, values.dtype),
        compiler_params=pltpu.CompilerParams(vmem_limit_bytes=ALL_VMEM),
        cost_estimate=pl.CostEstimate(
            flops=2 * hidden_t.size * down_weight.shape[1],
            bytes_accessed=4 * values.size,
            transcendentals=0,
        ),
        name="pack_values",
    )(owner, counts, down_weight, hidden_t, values)
    return packed.reshape(width // HEAD, span + 16, slots * HEAD)


def unpack(table, slots, span):
    heads, rows, _ = table.shape
    part, blocks, shape = pack_specs(slots, span, heads * HEAD, rows)
    return pl.pallas_call(
        unpack_kernel,
        grid=(PACK_STEPS,),
        in_specs=[blocks],
        out_specs=part,
        out_shape=jax.ShapeDtypeStruct((slots, span, heads * HEAD), table.dtype),
        compiler_params=pltpu.CompilerParams(vmem_limit_bytes=VMEM_LIMIT),
        cost_estimate=pl.CostEstimate(flops=0, bytes_accessed=4 * slots * span * heads * HEAD, transcendentals=0),
        name="unpack",
    )(table.reshape(shape))


STATS_CHUNK = 4
GRAD_CHUNK = 14


def two_sided(q_ref, u_ref):
    q, u = q_ref[0], u_ref[0]
    zero = jnp.zeros_like(q)
    return jnp.concatenate(
        [jnp.concatenate([q, zero], axis=1), jnp.concatenate([zero, u], axis=1)], axis=0
    )


def gathered(chosen_ref, k_ref, v_ref, slots, span, first):
    blocks = []
    for i in range(STATS_CHUNK):
        slot = chosen_ref[first + i]
        device, second = slot // slots, lax.rem(slot, slots) == 1
        k, v = k_ref[device, :span, :], v_ref[device, :span, :]
        left = jnp.concatenate([k[:, :HEAD], v[:, :HEAD]], axis=1)
        right = jnp.concatenate([k[:, HEAD:], v[:, HEAD:]], axis=1)
        blocks.append(jnp.where(second, right, left))
    return jnp.concatenate(blocks, axis=0)


def stats_kernel(
    per_question, slots, span, chosen_ref, q_ref, u_ref, k_ref, v_ref, o_ref, rows_ref
):
    question = pl.program_id(0)
    targets = q_ref.shape[2]
    both = two_sided(q_ref, u_ref)
    top = jnp.full((1, targets), -jnp.inf, F32)
    mass = jnp.zeros((1, targets), F32)
    dot = jnp.zeros((1, targets), F32)
    for chunk in range(per_question // STATS_CHUNK):
        first = question * per_question + chunk * STATS_CHUNK
        rows = gathered(chosen_ref, k_ref, v_ref, slots, span, first)
        rows_ref[0, chunk * STATS_CHUNK * span : (chunk + 1) * STATS_CHUNK * span, :] = rows
        prod = jnp.dot(rows, both, preferred_element_type=F32)
        scores, prob_grad = prod[:, :targets], prod[:, targets:]
        new_top = jnp.maximum(top, jnp.max(scores, axis=0, keepdims=True))
        scale = jnp.exp(top - new_top)
        exp_scores = jnp.exp(scores - new_top)
        mass = mass * scale + jnp.sum(exp_scores, axis=0, keepdims=True)
        dot = dot * scale + jnp.sum(exp_scores * prob_grad, axis=0, keepdims=True)
        top = new_top
    o_ref[0] = jnp.concatenate([top, mass, dot, jnp.zeros((5, targets), F32)], axis=0)


def row_stats(s_ref):
    members = s_ref.shape[0]
    tops = [s_ref[i, 0, 0:1, :] for i in range(members)]
    top = functools.reduce(jnp.maximum, tops)
    scales = [jnp.exp(t - top) for t in tops]
    inverse = 1.0 / sum(s_ref[i, 0, 1:2, :] * scales[i] for i in range(members))
    delta = sum(s_ref[i, 0, 2:3, :] * scales[i] for i in range(members)) * inverse
    return top, inverse, delta


def chunk_products(rows, both, stats):
    top, inverse, delta = stats
    targets = top.shape[1]
    prod = jnp.dot(rows, both, preferred_element_type=F32)
    scores, prob_grad = prod[:, :targets], prod[:, targets:]
    weights = jnp.exp(scores - top) * inverse
    score_grad = (weights * (prob_grad - delta)).astype(BF16)
    return weights, score_grad


def store_half(o_ref, slot, slots, value):
    device, span = slot // slots, value.shape[0]
    lanes = lax.broadcasted_iota(jnp.int32, value.shape, 1)
    old = o_ref[device, :span, :]
    o_ref[device, :span, :] = jnp.where(lanes // HEAD == lax.rem(slot, slots), value, old)


def query_value_kernel(
    per_question,
    slots,
    span,
    chosen_ref,
    q_ref,
    u_ref,
    w_ref,
    s_ref,
    rows_ref,
    dq_ref,
    o_ref,
    grad_ref,
):
    question = pl.program_id(0)
    targets = q_ref.shape[2]
    peers, _, pair_width = dq_ref.shape
    piece = targets // peers

    @pl.when(question == 0)
    def _():
        o_ref[...] = jnp.zeros_like(o_ref)

    both = two_sided(q_ref, u_ref)
    upstream = jnp.concatenate([u_ref[0]] * slots, axis=0)
    stats = row_stats(s_ref)
    size = GRAD_CHUNK * span
    last = (((1,), (1,)), ((), ()))
    for chunk in range(per_question // GRAD_CHUNK):
        first = question * per_question + chunk * GRAD_CHUNK
        rows = rows_ref[0, chunk * size : (chunk + 1) * size, :]
        weights, score_grad = chunk_products(rows, both, stats)
        grad_ref[chunk * size : (chunk + 1) * size, :] = score_grad
        out = lax.dot_general(
            weights.astype(BF16), upstream, last, preferred_element_type=F32
        ).astype(BF16)
        for i in range(GRAD_CHUNK):
            store_half(o_ref, chosen_ref[first + i], slots, out[i * span : (i + 1) * span])
    dq = lax.dot_general(
        rows_ref[0], grad_ref[...], (((0,), (0,)), ((), ())), preferred_element_type=F32
    )[:HEAD]

    for side in range(pair_width // piece):

        @pl.when(question % (pair_width // piece) == side)
        def _():
            for peer in range(peers):
                dq_ref[peer, :, side * piece : (side + 1) * piece] = dq[
                    :, peer * piece : (peer + 1) * piece
                ]

    high = dq.astype(BF16)
    low = (dq - high.astype(F32)).astype(BF16)
    latent = jnp.dot(w_ref[...], high, preferred_element_type=F32) + jnp.dot(
        w_ref[...], low, preferred_element_type=F32
    )
    latent = latent.astype(BF16)
    bands = latent.shape[0] // 8
    tiles = o_ref.shape[0] // bands
    for band in range(bands):
        for part in range(targets // 128):
            tile = band * tiles + question * (targets // 128) + part
            o_ref[tile, span:, :] = latent[
                band * 8 : (band + 1) * 8, part * 128 : (part + 1) * 128
            ]


def key_kernel(per_question, slots, span, chosen_ref, q_ref, u_ref, s_ref, rows_ref, o_ref):
    question = pl.program_id(0)

    @pl.when(question == 0)
    def _():
        o_ref[...] = jnp.zeros_like(o_ref)

    both = two_sided(q_ref, u_ref)
    query = jnp.concatenate([q_ref[0]] * slots, axis=0)
    stats = row_stats(s_ref)
    for chunk in range(per_question // GRAD_CHUNK):
        first = question * per_question + chunk * GRAD_CHUNK
        rows = rows_ref[0, chunk * GRAD_CHUNK * span : (chunk + 1) * GRAD_CHUNK * span, :]
        _, score_grad = chunk_products(rows, both, stats)
        out = lax.dot_general(
            score_grad, query, (((1,), (1,)), ((), ())), preferred_element_type=F32
        ).astype(BF16)
        for i in range(GRAD_CHUNK):
            store_half(o_ref, chosen_ref[first + i], slots, out[i * span : (i + 1) * span])


def attend_stats(chosen, query_t, upstream_t, key_table, value_table, per_question, slots, span):
    questions, size, targets = query_t.shape
    one = pl.BlockSpec((1, size, targets), lambda q, c: (q, 0, 0))
    tables = [
        pl.BlockSpec(table.shape, lambda q, c: (0, 0, 0)) for table in (key_table, value_table)
    ]
    keys = per_question * span
    return pl.pallas_call(
        functools.partial(stats_kernel, per_question, slots, span),
        grid_spec=pltpu.PrefetchScalarGridSpec(
            num_scalar_prefetch=1,
            grid=(questions,),
            in_specs=[one, one, *tables],
            out_specs=[
                pl.BlockSpec((1, 8, targets), lambda q, c: (q, 0, 0)),
                pl.BlockSpec((1, keys, 2 * size), lambda q, c: (q, 0, 0)),
            ],
        ),
        out_shape=[
            jax.ShapeDtypeStruct((questions, 8, targets), F32),
            jax.ShapeDtypeStruct((questions, keys, 2 * size), BF16),
        ],
        compiler_params=pltpu.CompilerParams(vmem_limit_bytes=VMEM_LIMIT),
        cost_estimate=pl.CostEstimate(
            flops=8 * questions * targets * keys * HEAD,
            bytes_accessed=4 * key_table.size,
            transcendentals=questions * targets * keys,
        ),
        name="stats",
    )(chosen, query_t, upstream_t, key_table, value_table)


def query_value_grads(
    chosen, query_t, upstream_t, up_weight, stats, rows, heads, per_question, slots, span
):
    questions, size, targets = query_t.shape
    peers = stats.shape[0]
    one = pl.BlockSpec((1, size, targets), lambda q, c: (q, 0, 0))
    whole = pl.BlockSpec((1,) + rows.shape[1:], lambda q, c: (q, 0, 0))
    out = (heads, span + 8, rows.shape[2])
    keys = per_question * span
    piece = targets // peers
    in_block = 128 // piece
    return pl.pallas_call(
        functools.partial(query_value_kernel, per_question, slots, span),
        grid_spec=pltpu.PrefetchScalarGridSpec(
            num_scalar_prefetch=1,
            grid=(questions,),
            in_specs=[
                one,
                one,
                pl.BlockSpec(up_weight.shape, lambda q, c: (0, 0)),
                pl.BlockSpec((peers, 1, 8, targets), lambda q, c: (0, q, 0, 0)),
                whole,
            ],
            out_specs=[
                pl.BlockSpec((peers, size, 128), lambda q, c: (0, 0, q // in_block)),
                pl.BlockSpec(out, lambda q, c: (0, 0, 0)),
            ],
            scratch_shapes=[pltpu.VMEM((keys, targets), BF16)],
        ),
        out_shape=[
            pltpu.HBM((peers, size, questions * piece), F32),
            pltpu.HBM(out, BF16),
        ],
        compiler_params=pltpu.CompilerParams(vmem_limit_bytes=VMEM_LIMIT),
        cost_estimate=pl.CostEstimate(
            flops=24 * questions * targets * keys * HEAD,
            bytes_accessed=4 * rows.size,
            transcendentals=questions * targets * keys,
        ),
        name="query_value_grads",
    )(chosen, query_t, upstream_t, up_weight, stats, rows)


def key_grads(chosen, query_t, upstream_t, stats, rows, heads, per_question, slots, span):
    questions, size, targets = query_t.shape
    peers = stats.shape[0]
    one = pl.BlockSpec((1, size, targets), lambda q, c: (q, 0, 0))
    whole = pl.BlockSpec((1,) + rows.shape[1:], lambda q, c: (q, 0, 0))
    out = (heads, span + 8, rows.shape[2])
    keys = per_question * span
    return pl.pallas_call(
        functools.partial(key_kernel, per_question, slots, span),
        grid_spec=pltpu.PrefetchScalarGridSpec(
            num_scalar_prefetch=1,
            grid=(questions,),
            in_specs=[
                one,
                one,
                pl.BlockSpec((peers, 1, 8, targets), lambda q, c: (0, q, 0, 0)),
                whole,
            ],
            out_specs=pl.BlockSpec(out, lambda q, c: (0, 0, 0)),
        ),
        out_shape=pltpu.HBM(out, BF16),
        compiler_params=pltpu.CompilerParams(vmem_limit_bytes=VMEM_LIMIT),
        cost_estimate=pl.CostEstimate(
            flops=16 * questions * targets * keys * HEAD,
            bytes_accessed=4 * rows.size,
            transcendentals=questions * targets * keys,
        ),
        name="key_grads",
    )(chosen, query_t, upstream_t, stats, rows)


def to_all(x, axis):
    size = lax.axis_size(axis)
    return exchange(
        jnp.broadcast_to(x[None], (size,) + x.shape), axis
    )


def scatter_sum_tp(x):
    size, here = lax.axis_size("tp"), lax.axis_index("tp")
    own = lax.dynamic_index_in_dim(x, here, 0, keepdims=False)
    for k in range(1, size):
        sent = lax.dynamic_index_in_dim(x, (here + k) % size, 0, keepdims=False)
        own = own + lax.ppermute(sent, "tp", [(i, (i + k) % size) for i in range(size)])
    return own


def exchange(x, axis):
    order = None
    if axis == "grp":
        size = lax.axis_size(axis)
        order = [[reverse(i, size) for i in range(size)]]
    return lax.all_to_all(
        x, axis, split_axis=0, concat_axis=0, tiled=True, axis_index_groups=order
    )


def with_tile(table, tile, row):
    tile = jnp.broadcast_to(tile[None], (table.shape[0],) + tile.shape)
    return lax.dynamic_update_slice(table, tile, (0, row, 0))


def untiled(x, tiles):
    bands, parts, rows, lanes = tiles
    return jnp.transpose(x.reshape(tiles), (0, 2, 1, 3)).reshape(bands * rows, parts * lanes)


def local(
    keys,
    values,
    frozen_query_projection,
    context_gradient,
    hidden,
    adapter_down_weight,
    adapter_up_weight,
    owner,
    counts,
    target_length,
):
    group_count, token_split = lax.axis_size("grp"), lax.axis_size("tp")
    questions, targets, _ = frozen_query_projection.shape
    slots_dev, span, _ = keys.shape
    total_slots = group_count * slots_dev
    per_question = (total_slots - group_count // 4) // questions
    piece = targets // token_split
    positions = questions * targets
    tiles = (HEAD // 8, positions // 128, 8, 128)

    hidden_t = jnp.swapaxes(hidden, 1, 2)
    value_table = exchange(
        pack_values(owner, counts, adapter_down_weight, hidden_t, values), "grp"
    )
    latent_tile = jnp.sum(value_table[:, span : span + 8, :].astype(F32), axis=0).astype(BF16)
    slot_key = value_table[:, span + 8, :slots_dev].astype(jnp.int32).reshape(total_slots)
    key_table = exchange(with_tile(pack_keys(keys, 8), latent_tile, span), "grp")

    slot_ids = jnp.arange(total_slots, dtype=jnp.int32)
    same = (slot_key[:, None] == slot_key[None, :]) & (slot_ids[None, :] < slot_ids[:, None])
    rank = jnp.sum(same.astype(jnp.int32), axis=1)
    place = slot_key * per_question + rank
    wanted = jnp.arange(questions * per_question, dtype=jnp.int32)
    hit = (place[None, :] == wanted[:, None]) & (slot_key < questions)[None, :]
    chosen = jnp.sum(jnp.where(hit, slot_ids[None, :], 0), axis=1)

    step_ids = lax.broadcasted_iota(jnp.int32, (questions, 1, targets), 2)
    keep = step_ids < target_length[:, None, None]
    upstream_t = jnp.swapaxes(context_gradient, 1, 2)
    upstream_t = jnp.where(keep, upstream_t, jnp.zeros_like(upstream_t))
    latent_t = untiled(key_table[:, span:, :], tiles).reshape(HEAD, questions, targets)
    raised = jnp.einsum("rd,rqt->qdt", adapter_up_weight, latent_t, preferred_element_type=F32)
    frozen_t = jnp.swapaxes(frozen_query_projection, 1, 2)
    query_t = (frozen_t.astype(F32) + raised).astype(BF16)

    sizes = (per_question, slots_dev, span)
    stats, rows = attend_stats(chosen, query_t, upstream_t, key_table, value_table, *sizes)
    all_stats = to_all(stats, "tp")
    dq_parts, value_grads = query_value_grads(
        chosen, query_t, upstream_t, adapter_up_weight, all_stats, rows, group_count, *sizes
    )
    grads = key_grads(chosen, query_t, upstream_t, all_stats, rows, group_count, *sizes)
    value_back = exchange(value_grads, "grp")
    latent_grad_tile = jnp.sum(value_back[:, span:, :].astype(F32), axis=0).astype(BF16)
    grad_values = unpack(value_back, slots_dev, span)
    key_back = exchange(with_tile(grads, latent_grad_tile, span), "grp")
    grad_keys = unpack(key_back, slots_dev, span)
    latent_grad = untiled(key_back[:, span:, :], tiles).reshape(HEAD, questions, targets)
    grad_a = jnp.einsum("qdt,rqt->dr", hidden_t, latent_grad, preferred_element_type=F32)

    dq_t = scatter_sum_tp(dq_parts).astype(BF16).reshape(HEAD, questions, piece)
    adapted = jnp.transpose(dq_t, (1, 2, 0))
    start = lax.axis_index("tp") * piece
    latent_cut = lax.dynamic_slice_in_dim(latent_t, start, piece, 2)
    grad_b = jnp.einsum("rqt,dqt->rd", latent_cut, dq_t, preferred_element_type=F32)
    got = to_all(jnp.concatenate([grad_a, grad_b], axis=1), ("sect", "tp"))
    got, grad_keys = lax.optimization_barrier((got, grad_keys))
    grads = jnp.sum(got, axis=0)
    return (adapted, grad_keys, grad_values, grads[:, :HEAD], grads[:, HEAD:])


def solution(mesh):
    return jax.shard_map(
        local,
        mesh=mesh,
        in_specs=(
            P(("sect", "grp"), "tp", None),
            P(("sect", "grp"), "tp", None),
            P("sect", None, "grp"),
            P("sect", None, "grp"),
            P("sect", None, "grp"),
            P("grp", None),
            P(None, "grp"),
            P(("sect", "grp")),
            P(("sect", "grp")),
            P("sect"),
        ),
        out_specs=(
            P("sect", "tp", "grp"),
            P(("sect", "grp"), "tp", None),
            P(("sect", "grp"), "tp", None),
            P("grp", None),
            P(None, "grp"),
        ),
        check_vma=False,
    )
```

```python
import functools

import jax
import jax.numpy as jnp
from jax import lax
from jax.experimental import pallas as pl
from jax.experimental.pallas import tpu as pltpu
from jax.sharding import PartitionSpec as P

HEAD = 64
BF16 = jnp.bfloat16
F32 = jnp.float32
VMEM_LIMIT = 32 * 1024 * 1024
ALL_VMEM = 62 * 1024 * 1024


ORDER = (4, 5, 2, 1, 3, 0)


def member_at(position):
    return sum(((position >> j) & 1) << bit for j, bit in enumerate(ORDER))


def position_of(member):
    return sum(((member >> bit) & 1) << j for j, bit in enumerate(ORDER))


PACK_STEPS = 2


def block_of(head):
    position = position_of(head)
    return position // 4, 0, position % 2


def pack_rows(x_ref, o_ref):
    slots, span, width = x_ref.shape
    for pair in range(width // (2 * HEAD)):
        low = pair * 2 * HEAD
        parts = [x_ref[slot, :, low : low + 2 * HEAD] for slot in range(slots)]
        for side in range(2):
            cut = slice(side * HEAD, (side + 1) * HEAD)
            o_ref[*block_of(2 * pair + side), :span, :] = jnp.concatenate(
                [part[:, cut] for part in parts], axis=1
            )


def pack_key_kernel(k_ref, o_ref):
    pack_rows(k_ref, o_ref)


def pack_value_kernel(owner_ref, counts_ref, down_ref, hidden_ref, v_ref, o_ref):
    pack_rows(v_ref, o_ref)
    span = v_ref.shape[1]
    questions, _, targets = hidden_ref.shape
    lanes = lax.broadcasted_iota(jnp.int32, (8, 128), 1)
    tags = jnp.zeros(lanes.shape, jnp.int32)
    for slot in range(owner_ref.shape[0]):
        tag = jnp.where(slot < counts_ref[0], owner_ref[slot], questions)
        tags = jnp.where(lanes == slot, tag, tags)
    tags = tags.astype(F32)
    down = down_ref[...]
    bands = down.shape[1] // 8
    outer, _, inner, _, _ = o_ref.shape
    turns, halves = outer // bands, targets // 128
    for turn in range(turns):
        for j in range(inner):
            part = (turn * PACK_STEPS + pl.program_id(0)) * inner + j
            start = pl.multiple_of(lax.rem(part, halves) * 128, 128)
            latent = lax.dot_general(
                down,
                hidden_ref[part // halves, :, pl.ds(start, 128)],
                (((0,), (0,)), ((), ())),
                preferred_element_type=F32,
            )
            for band in range(bands):
                tile = latent[band * 8 : (band + 1) * 8]
                o_ref[band * turns + turn, 0, j, span : span + 16, :] = jnp.concatenate(
                    [tile, tags], axis=0
                ).astype(o_ref.dtype)


def unpack_kernel(i_ref, o_ref):
    slots, span, width = o_ref.shape
    for pair in range(width // (2 * HEAD)):
        low = pair * 2 * HEAD
        even = i_ref[*block_of(2 * pair), :span, :]
        odd = i_ref[*block_of(2 * pair + 1), :span, :]
        for slot in range(slots):
            side = slice(slot * HEAD, (slot + 1) * HEAD)
            o_ref[slot, :, low : low + 2 * HEAD] = jnp.concatenate([even[:, side], odd[:, side]], axis=1)


def pack_specs(slots, span, width, rows):
    heads = width // HEAD
    shape = (heads // 4, PACK_STEPS, 2, rows, slots * HEAD)
    part = pl.BlockSpec((slots, span, width // PACK_STEPS), lambda i: (0, 0, i))
    table = pl.BlockSpec((shape[0], 1) + shape[2:], lambda i: (0, i, 0, 0, 0))
    return part, table, shape


def pack_keys(keys, spare):
    slots, span, width = keys.shape
    part, table, shape = pack_specs(slots, span, width, span + spare)
    packed = pl.pallas_call(
        pack_key_kernel,
        grid=(PACK_STEPS,),
        in_specs=[part],
        out_specs=table,
        out_shape=jax.ShapeDtypeStruct(shape, keys.dtype),
        compiler_params=pltpu.CompilerParams(vmem_limit_bytes=VMEM_LIMIT),
        cost_estimate=pl.CostEstimate(flops=0, bytes_accessed=4 * keys.size, transcendentals=0),
        name="pack_keys",
    )(keys)
    return packed.reshape(width // HEAD, span + spare, slots * HEAD)


def pack_values(owner, counts, down_weight, hidden_t, values):
    slots, span, width = values.shape
    part, table, shape = pack_specs(slots, span, width, span + 16)
    smem = pl.BlockSpec(memory_space=pltpu.SMEM)
    packed = pl.pallas_call(
        pack_value_kernel,
        grid=(PACK_STEPS,),
        in_specs=[
            smem,
            smem,
            pl.BlockSpec(down_weight.shape, lambda i: (0, 0)),
            pl.BlockSpec(hidden_t.shape, lambda i: (0, 0, 0)),
            part,
        ],
        out_specs=table,
        out_shape=jax.ShapeDtypeStruct(shape, values.dtype),
        compiler_params=pltpu.CompilerParams(vmem_limit_bytes=ALL_VMEM),
        cost_estimate=pl.CostEstimate(
            flops=2 * hidden_t.size * down_weight.shape[1],
            bytes_accessed=4 * values.size,
            transcendentals=0,
        ),
        name="pack_values",
    )(owner, counts, down_weight, hidden_t, values)
    return packed.reshape(width // HEAD, span + 16, slots * HEAD)


def unpack(table, slots, span):
    heads, rows, _ = table.shape
    part, blocks, shape = pack_specs(slots, span, heads * HEAD, rows)
    return pl.pallas_call(
        unpack_kernel,
        grid=(PACK_STEPS,),
        in_specs=[blocks],
        out_specs=part,
        out_shape=jax.ShapeDtypeStruct((slots, span, heads * HEAD), table.dtype),
        compiler_params=pltpu.CompilerParams(vmem_limit_bytes=VMEM_LIMIT),
        cost_estimate=pl.CostEstimate(flops=0, bytes_accessed=4 * slots * span * heads * HEAD, transcendentals=0),
        name="unpack",
    )(table.reshape(shape))


STATS_CHUNK = 4
GRAD_CHUNK = 14


def two_sided(q_ref, u_ref):
    q, u = q_ref[0], u_ref[0]
    zero = jnp.zeros_like(q)
    return jnp.concatenate(
        [jnp.concatenate([q, zero], axis=1), jnp.concatenate([zero, u], axis=1)], axis=0
    )


def gathered(chosen_ref, k_ref, v_ref, slots, span, first):
    blocks = []
    for i in range(STATS_CHUNK):
        slot = chosen_ref[first + i]
        device, second = slot // slots, lax.rem(slot, slots) == 1
        k, v = k_ref[device, :span, :], v_ref[device, :span, :]
        left = jnp.concatenate([k[:, :HEAD], v[:, :HEAD]], axis=1)
        right = jnp.concatenate([k[:, HEAD:], v[:, HEAD:]], axis=1)
        blocks.append(jnp.where(second, right, left))
    return jnp.concatenate(blocks, axis=0)


def stats_kernel(
    per_question, slots, span, chosen_ref, q_ref, u_ref, k_ref, v_ref, o_ref, rows_ref
):
    question = pl.program_id(0)
    targets = q_ref.shape[2]
    both = two_sided(q_ref, u_ref)
    top = jnp.full((1, targets), -jnp.inf, F32)
    mass = jnp.zeros((1, targets), F32)
    dot = jnp.zeros((1, targets), F32)
    for chunk in range(per_question // STATS_CHUNK):
        first = question * per_question + chunk * STATS_CHUNK
        rows = gathered(chosen_ref, k_ref, v_ref, slots, span, first)
        rows_ref[0, chunk * STATS_CHUNK * span : (chunk + 1) * STATS_CHUNK * span, :] = rows
        prod = jnp.dot(rows, both, preferred_element_type=F32)
        scores, prob_grad = prod[:, :targets], prod[:, targets:]
        new_top = jnp.maximum(top, jnp.max(scores, axis=0, keepdims=True))
        scale = jnp.exp(top - new_top)
        exp_scores = jnp.exp(scores - new_top)
        mass = mass * scale + jnp.sum(exp_scores, axis=0, keepdims=True)
        dot = dot * scale + jnp.sum(exp_scores * prob_grad, axis=0, keepdims=True)
        top = new_top
    o_ref[0] = jnp.concatenate([top, mass, dot, jnp.zeros((5, targets), F32)], axis=0)


def row_stats(s_ref):
    members = s_ref.shape[0]
    tops = [s_ref[i, 0, 0:1, :] for i in range(members)]
    top = functools.reduce(jnp.maximum, tops)
    scales = [jnp.exp(t - top) for t in tops]
    inverse = 1.0 / sum(s_ref[i, 0, 1:2, :] * scales[i] for i in range(members))
    delta = sum(s_ref[i, 0, 2:3, :] * scales[i] for i in range(members)) * inverse
    return top, inverse, delta


def chunk_products(rows, both, stats):
    top, inverse, delta = stats
    targets = top.shape[1]
    prod = jnp.dot(rows, both, preferred_element_type=F32)
    scores, prob_grad = prod[:, :targets], prod[:, targets:]
    weights = jnp.exp(scores - top) * inverse
    score_grad = (weights * (prob_grad - delta)).astype(BF16)
    return weights, score_grad


def store_half(o_ref, slot, slots, value):
    device, span = slot // slots, value.shape[0]
    lanes = lax.broadcasted_iota(jnp.int32, value.shape, 1)
    old = o_ref[device, :span, :]
    o_ref[device, :span, :] = jnp.where(lanes // HEAD == lax.rem(slot, slots), value, old)


def query_value_kernel(
    per_question,
    slots,
    span,
    chosen_ref,
    q_ref,
    u_ref,
    w_ref,
    s_ref,
    rows_ref,
    dq_ref,
    o_ref,
    grad_ref,
):
    question = pl.program_id(0)
    targets = q_ref.shape[2]
    peers, _, pair_width = dq_ref.shape
    piece = targets // peers

    @pl.when(question == 0)
    def _():
        o_ref[...] = jnp.zeros_like(o_ref)

    both = two_sided(q_ref, u_ref)
    upstream = jnp.concatenate([u_ref[0]] * slots, axis=0)
    stats = row_stats(s_ref)
    size = GRAD_CHUNK * span
    last = (((1,), (1,)), ((), ()))
    for chunk in range(per_question // GRAD_CHUNK):
        first = question * per_question + chunk * GRAD_CHUNK
        rows = rows_ref[0, chunk * size : (chunk + 1) * size, :]
        weights, score_grad = chunk_products(rows, both, stats)
        grad_ref[chunk * size : (chunk + 1) * size, :] = score_grad
        out = lax.dot_general(
            weights.astype(BF16), upstream, last, preferred_element_type=F32
        ).astype(BF16)
        for i in range(GRAD_CHUNK):
            store_half(o_ref, chosen_ref[first + i], slots, out[i * span : (i + 1) * span])
    dq = lax.dot_general(
        rows_ref[0], grad_ref[...], (((0,), (0,)), ((), ())), preferred_element_type=F32
    )[:HEAD]

    for side in range(pair_width // piece):

        @pl.when(question % (pair_width // piece) == side)
        def _():
            for peer in range(peers):
                dq_ref[peer, :, side * piece : (side + 1) * piece] = dq[
                    :, peer * piece : (peer + 1) * piece
                ]

    high = dq.astype(BF16)
    low = (dq - high.astype(F32)).astype(BF16)
    latent = jnp.dot(w_ref[...], high, preferred_element_type=F32) + jnp.dot(
        w_ref[...], low, preferred_element_type=F32
    )
    latent = latent.astype(BF16)
    bands = latent.shape[0] // 8
    tiles = o_ref.shape[0] // bands
    for band in range(bands):
        for part in range(targets // 128):
            tile = band * tiles + question * (targets // 128) + part
            o_ref[tile, span:, :] = latent[
                band * 8 : (band + 1) * 8, part * 128 : (part + 1) * 128
            ]


def key_kernel(per_question, slots, span, chosen_ref, q_ref, u_ref, s_ref, rows_ref, o_ref):
    question = pl.program_id(0)

    @pl.when(question == 0)
    def _():
        o_ref[...] = jnp.zeros_like(o_ref)

    both = two_sided(q_ref, u_ref)
    query = jnp.concatenate([q_ref[0]] * slots, axis=0)
    stats = row_stats(s_ref)
    for chunk in range(per_question // GRAD_CHUNK):
        first = question * per_question + chunk * GRAD_CHUNK
        rows = rows_ref[0, chunk * GRAD_CHUNK * span : (chunk + 1) * GRAD_CHUNK * span, :]
        _, score_grad = chunk_products(rows, both, stats)
        out = lax.dot_general(
            score_grad, query, (((1,), (1,)), ((), ())), preferred_element_type=F32
        ).astype(BF16)
        for i in range(GRAD_CHUNK):
            store_half(o_ref, chosen_ref[first + i], slots, out[i * span : (i + 1) * span])


def attend_stats(chosen, query_t, upstream_t, key_table, value_table, per_question, slots, span):
    questions, size, targets = query_t.shape
    one = pl.BlockSpec((1, size, targets), lambda q, c: (q, 0, 0))
    tables = [
        pl.BlockSpec(table.shape, lambda q, c: (0, 0, 0)) for table in (key_table, value_table)
    ]
    keys = per_question * span
    return pl.pallas_call(
        functools.partial(stats_kernel, per_question, slots, span),
        grid_spec=pltpu.PrefetchScalarGridSpec(
            num_scalar_prefetch=1,
            grid=(questions,),
            in_specs=[one, one, *tables],
            out_specs=[
                pl.BlockSpec((1, 8, targets), lambda q, c: (q, 0, 0)),
                pl.BlockSpec((1, keys, 2 * size), lambda q, c: (q, 0, 0)),
            ],
        ),
        out_shape=[
            jax.ShapeDtypeStruct((questions, 8, targets), F32),
            jax.ShapeDtypeStruct((questions, keys, 2 * size), BF16),
        ],
        compiler_params=pltpu.CompilerParams(vmem_limit_bytes=VMEM_LIMIT),
        cost_estimate=pl.CostEstimate(
            flops=8 * questions * targets * keys * HEAD,
            bytes_accessed=4 * key_table.size,
            transcendentals=questions * targets * keys,
        ),
        name="stats",
    )(chosen, query_t, upstream_t, key_table, value_table)


def query_value_grads(
    chosen, query_t, upstream_t, up_weight, stats, rows, heads, per_question, slots, span
):
    questions, size, targets = query_t.shape
    peers = stats.shape[0]
    one = pl.BlockSpec((1, size, targets), lambda q, c: (q, 0, 0))
    whole = pl.BlockSpec((1,) + rows.shape[1:], lambda q, c: (q, 0, 0))
    out = (heads, span + 8, rows.shape[2])
    keys = per_question * span
    piece = targets // peers
    in_block = 128 // piece
    return pl.pallas_call(
        functools.partial(query_value_kernel, per_question, slots, span),
        grid_spec=pltpu.PrefetchScalarGridSpec(
            num_scalar_prefetch=1,
            grid=(questions,),
            in_specs=[
                one,
                one,
                pl.BlockSpec(up_weight.shape, lambda q, c: (0, 0)),
                pl.BlockSpec((peers, 1, 8, targets), lambda q, c: (0, q, 0, 0)),
                whole,
            ],
            out_specs=[
                pl.BlockSpec((peers, size, 128), lambda q, c: (0, 0, q // in_block)),
                pl.BlockSpec(out, lambda q, c: (0, 0, 0)),
            ],
            scratch_shapes=[pltpu.VMEM((keys, targets), BF16)],
        ),
        out_shape=[
            pltpu.HBM((peers, size, questions * piece), F32),
            pltpu.HBM(out, BF16),
        ],
        compiler_params=pltpu.CompilerParams(vmem_limit_bytes=VMEM_LIMIT),
        cost_estimate=pl.CostEstimate(
            flops=24 * questions * targets * keys * HEAD,
            bytes_accessed=4 * rows.size,
            transcendentals=questions * targets * keys,
        ),
        name="query_value_grads",
    )(chosen, query_t, upstream_t, up_weight, stats, rows)


def key_grads(chosen, query_t, upstream_t, stats, rows, heads, per_question, slots, span):
    questions, size, targets = query_t.shape
    peers = stats.shape[0]
    one = pl.BlockSpec((1, size, targets), lambda q, c: (q, 0, 0))
    whole = pl.BlockSpec((1,) + rows.shape[1:], lambda q, c: (q, 0, 0))
    out = (heads, span + 8, rows.shape[2])
    keys = per_question * span
    return pl.pallas_call(
        functools.partial(key_kernel, per_question, slots, span),
        grid_spec=pltpu.PrefetchScalarGridSpec(
            num_scalar_prefetch=1,
            grid=(questions,),
            in_specs=[
                one,
                one,
                pl.BlockSpec((peers, 1, 8, targets), lambda q, c: (0, q, 0, 0)),
                whole,
            ],
            out_specs=pl.BlockSpec(out, lambda q, c: (0, 0, 0)),
        ),
        out_shape=pltpu.HBM(out, BF16),
        compiler_params=pltpu.CompilerParams(vmem_limit_bytes=VMEM_LIMIT),
        cost_estimate=pl.CostEstimate(
            flops=16 * questions * targets * keys * HEAD,
            bytes_accessed=4 * rows.size,
            transcendentals=questions * targets * keys,
        ),
        name="key_grads",
    )(chosen, query_t, upstream_t, stats, rows)


def to_all(x, axis):
    size = lax.axis_size(axis)
    return exchange(
        jnp.broadcast_to(x[None], (size,) + x.shape), axis
    )


def scatter_sum_tp(x):
    size, here = lax.axis_size("tp"), lax.axis_index("tp")
    own = lax.dynamic_index_in_dim(x, here, 0, keepdims=False)
    for k in range(1, size):
        sent = lax.dynamic_index_in_dim(x, (here + k) % size, 0, keepdims=False)
        own = own + lax.ppermute(sent, "tp", [(i, (i + k) % size) for i in range(size)])
    return own


def exchange(x, axis):
    order = None
    if axis == "grp":
        size = lax.axis_size(axis)
        order = [[member_at(i) for i in range(size)]]
    return lax.all_to_all(
        x, axis, split_axis=0, concat_axis=0, tiled=True, axis_index_groups=order
    )


def with_tile(table, tile, row):
    tile = jnp.broadcast_to(tile[None], (table.shape[0],) + tile.shape)
    return lax.dynamic_update_slice(table, tile, (0, row, 0))


def untiled(x, tiles):
    bands, parts, rows, lanes = tiles
    return jnp.transpose(x.reshape(tiles), (0, 2, 1, 3)).reshape(bands * rows, parts * lanes)


def local(
    keys,
    values,
    frozen_query_projection,
    context_gradient,
    hidden,
    adapter_down_weight,
    adapter_up_weight,
    owner,
    counts,
    target_length,
):
    group_count, token_split = lax.axis_size("grp"), lax.axis_size("tp")
    questions, targets, _ = frozen_query_projection.shape
    slots_dev, span, _ = keys.shape
    total_slots = group_count * slots_dev
    per_question = (total_slots - group_count // 4) // questions
    piece = targets // token_split
    positions = questions * targets
    tiles = (HEAD // 8, positions // 128, 8, 128)

    hidden_t = jnp.swapaxes(hidden, 1, 2)
    value_table = exchange(
        pack_values(owner, counts, adapter_down_weight, hidden_t, values), "grp"
    )
    latent_tile = jnp.sum(value_table[:, span : span + 8, :].astype(F32), axis=0).astype(BF16)
    slot_key = value_table[:, span + 8, :slots_dev].astype(jnp.int32).reshape(total_slots)
    key_table = exchange(with_tile(pack_keys(keys, 8), latent_tile, span), "grp")

    slot_ids = jnp.arange(total_slots, dtype=jnp.int32)
    same = (slot_key[:, None] == slot_key[None, :]) & (slot_ids[None, :] < slot_ids[:, None])
    rank = jnp.sum(same.astype(jnp.int32), axis=1)
    place = slot_key * per_question + rank
    wanted = jnp.arange(questions * per_question, dtype=jnp.int32)
    hit = (place[None, :] == wanted[:, None]) & (slot_key < questions)[None, :]
    chosen = jnp.sum(jnp.where(hit, slot_ids[None, :], 0), axis=1)

    step_ids = lax.broadcasted_iota(jnp.int32, (questions, 1, targets), 2)
    keep = step_ids < target_length[:, None, None]
    upstream_t = jnp.swapaxes(context_gradient, 1, 2)
    upstream_t = jnp.where(keep, upstream_t, jnp.zeros_like(upstream_t))
    latent_t = untiled(key_table[:, span:, :], tiles).reshape(HEAD, questions, targets)
    raised = jnp.einsum("rd,rqt->qdt", adapter_up_weight, latent_t, preferred_element_type=F32)
    frozen_t = jnp.swapaxes(frozen_query_projection, 1, 2)
    query_t = (frozen_t.astype(F32) + raised).astype(BF16)

    sizes = (per_question, slots_dev, span)
    stats, rows = attend_stats(chosen, query_t, upstream_t, key_table, value_table, *sizes)
    all_stats = to_all(stats, "tp")
    dq_parts, value_grads = query_value_grads(
        chosen, query_t, upstream_t, adapter_up_weight, all_stats, rows, group_count, *sizes
    )
    grads = key_grads(chosen, query_t, upstream_t, all_stats, rows, group_count, *sizes)
    value_back = exchange(value_grads, "grp")
    latent_grad_tile = jnp.sum(value_back[:, span:, :].astype(F32), axis=0).astype(BF16)
    grad_values = unpack(value_back, slots_dev, span)
    key_back = exchange(with_tile(grads, latent_grad_tile, span), "grp")
    grad_keys = unpack(key_back, slots_dev, span)
    latent_grad = untiled(key_back[:, span:, :], tiles).reshape(HEAD, questions, targets)
    grad_a = jnp.einsum("qdt,rqt->dr", hidden_t, latent_grad, preferred_element_type=F32)

    dq_t = scatter_sum_tp(dq_parts).astype(BF16).reshape(HEAD, questions, piece)
    adapted = jnp.transpose(dq_t, (1, 2, 0))
    start = lax.axis_index("tp") * piece
    latent_cut = lax.dynamic_slice_in_dim(latent_t, start, piece, 2)
    grad_b = jnp.einsum("rqt,dqt->rd", latent_cut, dq_t, preferred_element_type=F32)
    got = to_all(jnp.concatenate([grad_a, grad_b], axis=1), ("sect", "tp"))
    got, grad_keys = lax.optimization_barrier((got, grad_keys))
    grads = jnp.sum(got, axis=0)
    return (adapted, grad_keys, grad_values, grads[:, :HEAD], grads[:, HEAD:])


def solution(mesh):
    return jax.shard_map(
        local,
        mesh=mesh,
        in_specs=(
            P(("sect", "grp"), "tp", None),
            P(("sect", "grp"), "tp", None),
            P("sect", None, "grp"),
            P("sect", None, "grp"),
            P("sect", None, "grp"),
            P("grp", None),
            P(None, "grp"),
            P(("sect", "grp")),
            P(("sect", "grp")),
            P("sect"),
        ),
        out_specs=(
            P("sect", "tp", "grp"),
            P(("sect", "grp"), "tp", None),
            P(("sect", "grp"), "tp", None),
            P("grp", None),
            P(None, "grp"),
        ),
        check_vma=False,
    )
```

```python
import functools

import jax
import jax.numpy as jnp
from jax import lax
from jax.experimental import pallas as pl
from jax.experimental.pallas import tpu as pltpu
from jax.sharding import PartitionSpec as P

HEAD = 64
BF16 = jnp.bfloat16
F32 = jnp.float32
VMEM_LIMIT = 32 * 1024 * 1024
ALL_VMEM = 62 * 1024 * 1024


ORDER = (4, 5, 2, 1, 3, 0)


def member_at(position):
    return sum(((position >> j) & 1) << bit for j, bit in enumerate(ORDER))


def position_of(member):
    return sum(((member >> bit) & 1) << j for j, bit in enumerate(ORDER))


PACK_STEPS = 2


def block_of(head):
    position = position_of(head)
    return position // 4, 0, position % 2


def pack_rows(x_ref, o_ref):
    slots, span, width = x_ref.shape
    for pair in range(width // (2 * HEAD)):
        low = pair * 2 * HEAD
        parts = [x_ref[slot, :, low : low + 2 * HEAD] for slot in range(slots)]
        for side in range(2):
            cut = slice(side * HEAD, (side + 1) * HEAD)
            o_ref[*block_of(2 * pair + side), :span, :] = jnp.concatenate(
                [part[:, cut] for part in parts], axis=1
            )


def pack_key_kernel(k_ref, o_ref):
    pack_rows(k_ref, o_ref)


def pack_value_kernel(owner_ref, counts_ref, down_ref, hidden_ref, v_ref, o_ref):
    pack_rows(v_ref, o_ref)
    span = v_ref.shape[1]
    questions, _, targets = hidden_ref.shape
    lanes = lax.broadcasted_iota(jnp.int32, (8, 128), 1)
    tags = jnp.zeros(lanes.shape, jnp.int32)
    for slot in range(owner_ref.shape[0]):
        tag = jnp.where(slot < counts_ref[0], owner_ref[slot], questions)
        tags = jnp.where(lanes == slot, tag, tags)
    tags = tags.astype(F32)
    down = down_ref[...]
    bands = down.shape[1] // 8
    outer, _, inner, _, _ = o_ref.shape
    turns, halves = outer // bands, targets // 128
    for turn in range(turns):
        for j in range(inner):
            part = (turn * PACK_STEPS + pl.program_id(0)) * inner + j
            start = pl.multiple_of(lax.rem(part, halves) * 128, 128)
            latent = lax.dot_general(
                down,
                hidden_ref[part // halves, :, pl.ds(start, 128)],
                (((0,), (0,)), ((), ())),
                preferred_element_type=F32,
            )
            for band in range(bands):
                tile = latent[band * 8 : (band + 1) * 8]
                o_ref[band * turns + turn, 0, j, span : span + 16, :] = jnp.concatenate(
                    [tile, tags], axis=0
                ).astype(o_ref.dtype)


def unpack_kernel(i_ref, o_ref):
    slots, span, width = o_ref.shape
    for pair in range(width // (2 * HEAD)):
        low = pair * 2 * HEAD
        even = i_ref[*block_of(2 * pair), :span, :]
        odd = i_ref[*block_of(2 * pair + 1), :span, :]
        for slot in range(slots):
            side = slice(slot * HEAD, (slot + 1) * HEAD)
            o_ref[slot, :, low : low + 2 * HEAD] = jnp.concatenate([even[:, side], odd[:, side]], axis=1)


def pack_specs(slots, span, width, rows):
    heads = width // HEAD
    shape = (heads // 4, PACK_STEPS, 2, rows, slots * HEAD)
    part = pl.BlockSpec((slots, span, width // PACK_STEPS), lambda i: (0, 0, i))
    table = pl.BlockSpec((shape[0], 1) + shape[2:], lambda i: (0, i, 0, 0, 0))
    return part, table, shape


def pack_keys(keys, spare):
    slots, span, width = keys.shape
    part, table, shape = pack_specs(slots, span, width, span + spare)
    packed = pl.pallas_call(
        pack_key_kernel,
        grid=(PACK_STEPS,),
        in_specs=[part],
        out_specs=table,
        out_shape=jax.ShapeDtypeStruct(shape, keys.dtype),
        compiler_params=pltpu.CompilerParams(vmem_limit_bytes=VMEM_LIMIT),
        cost_estimate=pl.CostEstimate(flops=0, bytes_accessed=4 * keys.size, transcendentals=0),
        name="pack_keys",
    )(keys)
    return packed.reshape(width // HEAD, span + spare, slots * HEAD)


def pack_values(owner, counts, down_weight, hidden_t, values):
    slots, span, width = values.shape
    part, table, shape = pack_specs(slots, span, width, span + 16)
    smem = pl.BlockSpec(memory_space=pltpu.SMEM)
    packed = pl.pallas_call(
        pack_value_kernel,
        grid=(PACK_STEPS,),
        in_specs=[
            smem,
            smem,
            pl.BlockSpec(down_weight.shape, lambda i: (0, 0)),
            pl.BlockSpec(hidden_t.shape, lambda i: (0, 0, 0)),
            part,
        ],
        out_specs=table,
        out_shape=jax.ShapeDtypeStruct(shape, values.dtype),
        compiler_params=pltpu.CompilerParams(vmem_limit_bytes=ALL_VMEM),
        cost_estimate=pl.CostEstimate(
            flops=2 * hidden_t.size * down_weight.shape[1],
            bytes_accessed=4 * values.size,
            transcendentals=0,
        ),
        name="pack_values",
    )(owner, counts, down_weight, hidden_t, values)
    return packed.reshape(width // HEAD, span + 16, slots * HEAD)


def unpack(table, slots, span):
    heads, rows, _ = table.shape
    part, blocks, shape = pack_specs(slots, span, heads * HEAD, rows)
    return pl.pallas_call(
        unpack_kernel,
        grid=(PACK_STEPS,),
        in_specs=[blocks],
        out_specs=part,
        out_shape=jax.ShapeDtypeStruct((slots, span, heads * HEAD), table.dtype),
        compiler_params=pltpu.CompilerParams(vmem_limit_bytes=VMEM_LIMIT),
        cost_estimate=pl.CostEstimate(flops=0, bytes_accessed=4 * slots * span * heads * HEAD, transcendentals=0),
        name="unpack",
    )(table.reshape(shape))


STATS_CHUNK = 2
GRAD_CHUNK = 28


def two_sided(q_ref, u_ref):
    q, u = q_ref[0], u_ref[0]
    zero = jnp.zeros_like(q)
    return jnp.concatenate(
        [jnp.concatenate([q, zero], axis=1), jnp.concatenate([zero, u], axis=1)], axis=0
    )


def gathered(chosen_ref, k_ref, v_ref, slots, span, first):
    blocks = []
    for i in range(STATS_CHUNK):
        slot = chosen_ref[first + i]
        device, second = slot // slots, lax.rem(slot, slots) == 1
        k, v = k_ref[device, :span, :], v_ref[device, :span, :]
        left = jnp.concatenate([k[:, :HEAD], v[:, :HEAD]], axis=1)
        right = jnp.concatenate([k[:, HEAD:], v[:, HEAD:]], axis=1)
        blocks.append(jnp.where(second, right, left))
    return jnp.concatenate(blocks, axis=0)


def stats_kernel(
    per_question, slots, span, chosen_ref, q_ref, u_ref, k_ref, v_ref, o_ref, rows_ref
):
    question = pl.program_id(0)
    targets = q_ref.shape[2]
    both = two_sided(q_ref, u_ref)
    top = jnp.full((1, targets), -jnp.inf, F32)
    mass = jnp.zeros((1, targets), F32)
    dot = jnp.zeros((1, targets), F32)
    for chunk in range(per_question // STATS_CHUNK):
        first = question * per_question + chunk * STATS_CHUNK
        rows = gathered(chosen_ref, k_ref, v_ref, slots, span, first)
        rows_ref[0, chunk * STATS_CHUNK * span : (chunk + 1) * STATS_CHUNK * span, :] = rows
        prod = jnp.dot(rows, both, preferred_element_type=F32)
        scores, prob_grad = prod[:, :targets], prod[:, targets:]
        new_top = jnp.maximum(top, jnp.max(scores, axis=0, keepdims=True))
        scale = jnp.exp(top - new_top)
        exp_scores = jnp.exp(scores - new_top)
        mass = mass * scale + jnp.sum(exp_scores, axis=0, keepdims=True)
        dot = dot * scale + jnp.sum(exp_scores * prob_grad, axis=0, keepdims=True)
        top = new_top

    @pl.when(question == 0)
    def _():
        o_ref[...] = jnp.zeros_like(o_ref)

    for i, row in enumerate((top, mass, dot)):
        o_ref[pl.ds(i * pl.num_programs(0) + question, 1), :] = row


def row_stats(s_ref):
    members, question = s_ref.shape[0], pl.program_id(0)
    tops, masses, dots = [
        [s_ref[m, pl.ds(i * pl.num_programs(0) + question, 1), :] for m in range(members)]
        for i in range(3)
    ]
    top = functools.reduce(jnp.maximum, tops)
    scales = [jnp.exp(t - top) for t in tops]
    inverse = 1.0 / sum(masses[i] * scales[i] for i in range(members))
    delta = sum(dots[i] * scales[i] for i in range(members)) * inverse
    return top, inverse, delta


def chunk_products(rows, both, stats):
    top, inverse, delta = stats
    targets = top.shape[1]
    prod = jnp.dot(rows, both, preferred_element_type=F32)
    scores, prob_grad = prod[:, :targets], prod[:, targets:]
    weights = jnp.exp(scores - top) * inverse
    score_grad = (weights * (prob_grad - delta)).astype(BF16)
    return weights, score_grad


def store_half(o_ref, slot, slots, value):
    device, span = slot // slots, value.shape[0]
    lanes = lax.broadcasted_iota(jnp.int32, value.shape, 1)
    old = o_ref[device, :span, :]
    o_ref[device, :span, :] = jnp.where(lanes // HEAD == lax.rem(slot, slots), value, old)


def query_value_kernel(
    per_question,
    slots,
    span,
    chosen_ref,
    q_ref,
    u_ref,
    w_ref,
    s_ref,
    rows_ref,
    dq_ref,
    o_ref,
    grad_ref,
):
    question = pl.program_id(0)
    targets = q_ref.shape[2]
    peers, _, pair_width = dq_ref.shape
    piece = targets // peers

    @pl.when(question == 0)
    def _():
        o_ref[...] = jnp.zeros_like(o_ref)

    both = two_sided(q_ref, u_ref)
    upstream = jnp.concatenate([u_ref[0]] * slots, axis=0)
    stats = row_stats(s_ref)
    size = GRAD_CHUNK * span
    last = (((1,), (1,)), ((), ()))
    for chunk in range(per_question // GRAD_CHUNK):
        first = question * per_question + chunk * GRAD_CHUNK
        rows = rows_ref[0, chunk * size : (chunk + 1) * size, :]
        weights, score_grad = chunk_products(rows, both, stats)
        grad_ref[chunk * size : (chunk + 1) * size, :] = score_grad
        out = lax.dot_general(
            weights.astype(BF16), upstream, last, preferred_element_type=F32
        ).astype(BF16)
        for i in range(GRAD_CHUNK):
            store_half(o_ref, chosen_ref[first + i], slots, out[i * span : (i + 1) * span])
    dq = lax.dot_general(
        rows_ref[0], grad_ref[...], (((0,), (0,)), ((), ())), preferred_element_type=F32
    )[:HEAD]

    for side in range(pair_width // piece):

        @pl.when(question % (pair_width // piece) == side)
        def _():
            for peer in range(peers):
                dq_ref[peer, :, side * piece : (side + 1) * piece] = dq[
                    :, peer * piece : (peer + 1) * piece
                ]

    high = dq.astype(BF16)
    low = (dq - high.astype(F32)).astype(BF16)
    latent = jnp.dot(w_ref[...], high, preferred_element_type=F32) + jnp.dot(
        w_ref[...], low, preferred_element_type=F32
    )
    latent = latent.astype(BF16)
    bands = latent.shape[0] // 8
    tiles = o_ref.shape[0] // bands
    for band in range(bands):
        for part in range(targets // 128):
            tile = band * tiles + question * (targets // 128) + part
            o_ref[tile, span:, :] = latent[
                band * 8 : (band + 1) * 8, part * 128 : (part + 1) * 128
            ]


def key_kernel(per_question, slots, span, chosen_ref, q_ref, u_ref, s_ref, rows_ref, o_ref):
    question = pl.program_id(0)

    @pl.when(question == 0)
    def _():
        o_ref[...] = jnp.zeros_like(o_ref)

    both = two_sided(q_ref, u_ref)
    query = jnp.concatenate([q_ref[0]] * slots, axis=0)
    stats = row_stats(s_ref)
    for chunk in range(per_question // GRAD_CHUNK):
        first = question * per_question + chunk * GRAD_CHUNK
        rows = rows_ref[0, chunk * GRAD_CHUNK * span : (chunk + 1) * GRAD_CHUNK * span, :]
        _, score_grad = chunk_products(rows, both, stats)
        out = lax.dot_general(
            score_grad, query, (((1,), (1,)), ((), ())), preferred_element_type=F32
        ).astype(BF16)
        for i in range(GRAD_CHUNK):
            store_half(o_ref, chosen_ref[first + i], slots, out[i * span : (i + 1) * span])


def attend_stats(chosen, query_t, upstream_t, key_table, value_table, per_question, slots, span):
    questions, size, targets = query_t.shape
    one = pl.BlockSpec((1, size, targets), lambda q, c: (q, 0, 0))
    stat_rows = -(-3 * questions // 8) * 8
    tables = [
        pl.BlockSpec(table.shape, lambda q, c: (0, 0, 0)) for table in (key_table, value_table)
    ]
    keys = per_question * span
    return pl.pallas_call(
        functools.partial(stats_kernel, per_question, slots, span),
        grid_spec=pltpu.PrefetchScalarGridSpec(
            num_scalar_prefetch=1,
            grid=(questions,),
            in_specs=[one, one, *tables],
            out_specs=[
                pl.BlockSpec((stat_rows, targets), lambda q, c: (0, 0)),
                pl.BlockSpec((1, keys, 2 * size), lambda q, c: (q, 0, 0)),
            ],
        ),
        out_shape=[
            jax.ShapeDtypeStruct((stat_rows, targets), F32),
            jax.ShapeDtypeStruct((questions, keys, 2 * size), BF16),
        ],
        compiler_params=pltpu.CompilerParams(vmem_limit_bytes=VMEM_LIMIT),
        cost_estimate=pl.CostEstimate(
            flops=8 * questions * targets * keys * HEAD,
            bytes_accessed=4 * key_table.size,
            transcendentals=questions * targets * keys,
        ),
        name="stats",
    )(chosen, query_t, upstream_t, key_table, value_table)


def query_value_grads(
    chosen, query_t, upstream_t, up_weight, stats, rows, heads, per_question, slots, span
):
    questions, size, targets = query_t.shape
    peers = stats.shape[0]
    one = pl.BlockSpec((1, size, targets), lambda q, c: (q, 0, 0))
    whole = pl.BlockSpec((1,) + rows.shape[1:], lambda q, c: (q, 0, 0))
    out = (heads, span + 8, rows.shape[2])
    keys = per_question * span
    piece = targets // peers
    in_block = 128 // piece
    return pl.pallas_call(
        functools.partial(query_value_kernel, per_question, slots, span),
        grid_spec=pltpu.PrefetchScalarGridSpec(
            num_scalar_prefetch=1,
            grid=(questions,),
            in_specs=[
                one,
                one,
                pl.BlockSpec(up_weight.shape, lambda q, c: (0, 0)),
                pl.BlockSpec(stats.shape, lambda q, c: (0, 0, 0)),
                whole,
            ],
            out_specs=[
                pl.BlockSpec((peers, size, 128), lambda q, c: (0, 0, q // in_block)),
                pl.BlockSpec(out, lambda q, c: (0, 0, 0)),
            ],
            scratch_shapes=[pltpu.VMEM((keys, targets), BF16)],
        ),
        out_shape=[
            pltpu.HBM((peers, size, questions * piece), F32),
            pltpu.HBM(out, BF16),
        ],
        compiler_params=pltpu.CompilerParams(vmem_limit_bytes=VMEM_LIMIT),
        cost_estimate=pl.CostEstimate(
            flops=24 * questions * targets * keys * HEAD,
            bytes_accessed=4 * rows.size,
            transcendentals=questions * targets * keys,
        ),
        name="query_value_grads",
    )(chosen, query_t, upstream_t, up_weight, stats, rows)


def key_grads(chosen, query_t, upstream_t, stats, rows, heads, per_question, slots, span):
    questions, size, targets = query_t.shape
    peers = stats.shape[0]
    one = pl.BlockSpec((1, size, targets), lambda q, c: (q, 0, 0))
    whole = pl.BlockSpec((1,) + rows.shape[1:], lambda q, c: (q, 0, 0))
    out = (heads, span + 8, rows.shape[2])
    keys = per_question * span
    return pl.pallas_call(
        functools.partial(key_kernel, per_question, slots, span),
        grid_spec=pltpu.PrefetchScalarGridSpec(
            num_scalar_prefetch=1,
            grid=(questions,),
            in_specs=[
                one,
                one,
                pl.BlockSpec(stats.shape, lambda q, c: (0, 0, 0)),
                whole,
            ],
            out_specs=pl.BlockSpec(out, lambda q, c: (0, 0, 0)),
        ),
        out_shape=pltpu.HBM(out, BF16),
        compiler_params=pltpu.CompilerParams(vmem_limit_bytes=VMEM_LIMIT),
        cost_estimate=pl.CostEstimate(
            flops=16 * questions * targets * keys * HEAD,
            bytes_accessed=4 * rows.size,
            transcendentals=questions * targets * keys,
        ),
        name="key_grads",
    )(chosen, query_t, upstream_t, stats, rows)


def to_all(x, axis):
    size = lax.axis_size(axis)
    return exchange(
        jnp.broadcast_to(x[None], (size,) + x.shape), axis
    )


def scatter_sum_tp(x):
    size, here = lax.axis_size("tp"), lax.axis_index("tp")
    own = lax.dynamic_index_in_dim(x, here, 0, keepdims=False)
    for k in range(1, size):
        sent = lax.dynamic_index_in_dim(x, (here + k) % size, 0, keepdims=False)
        own = own + lax.ppermute(sent, "tp", [(i, (i + k) % size) for i in range(size)])
    return own


def exchange(x, axis):
    order = None
    if axis == "grp":
        size = lax.axis_size(axis)
        order = [[member_at(i) for i in range(size)]]
    return lax.all_to_all(
        x, axis, split_axis=0, concat_axis=0, tiled=True, axis_index_groups=order
    )


def with_tile(table, tile, row):
    tile = jnp.broadcast_to(tile[None], (table.shape[0],) + tile.shape)
    return lax.dynamic_update_slice(table, tile, (0, row, 0))


def untiled(x, tiles):
    bands, parts, rows, lanes = tiles
    return jnp.transpose(x.reshape(tiles), (0, 2, 1, 3)).reshape(bands * rows, parts * lanes)


def local(
    keys,
    values,
    frozen_query_projection,
    context_gradient,
    hidden,
    adapter_down_weight,
    adapter_up_weight,
    owner,
    counts,
    target_length,
):
    group_count, token_split = lax.axis_size("grp"), lax.axis_size("tp")
    questions, targets, _ = frozen_query_projection.shape
    slots_dev, span, _ = keys.shape
    total_slots = group_count * slots_dev
    per_question = (total_slots - group_count // 4) // questions
    piece = targets // token_split
    positions = questions * targets
    tiles = (HEAD // 8, positions // 128, 8, 128)

    hidden_t = jnp.swapaxes(hidden, 1, 2)
    value_table = exchange(
        pack_values(owner, counts, adapter_down_weight, hidden_t, values), "grp"
    )
    latent_tile = jnp.sum(value_table[:, span : span + 8, :].astype(F32), axis=0).astype(BF16)
    slot_key = value_table[:, span + 8, :slots_dev].astype(jnp.int32).reshape(total_slots)
    key_table = exchange(with_tile(pack_keys(keys, 8), latent_tile, span), "grp")

    slot_ids = jnp.arange(total_slots, dtype=jnp.int32)
    same = (slot_key[:, None] == slot_key[None, :]) & (slot_ids[None, :] < slot_ids[:, None])
    rank = jnp.sum(same.astype(jnp.int32), axis=1)
    place = slot_key * per_question + rank
    wanted = jnp.arange(questions * per_question, dtype=jnp.int32)
    hit = (place[None, :] == wanted[:, None]) & (slot_key < questions)[None, :]
    chosen = jnp.sum(jnp.where(hit, slot_ids[None, :], 0), axis=1)

    step_ids = lax.broadcasted_iota(jnp.int32, (questions, 1, targets), 2)
    keep = step_ids < target_length[:, None, None]
    upstream_t = jnp.swapaxes(context_gradient, 1, 2)
    upstream_t = jnp.where(keep, upstream_t, jnp.zeros_like(upstream_t))
    latent_t = untiled(key_table[:, span:, :], tiles).reshape(HEAD, questions, targets)
    raised = jnp.einsum("rd,rqt->qdt", adapter_up_weight, latent_t, preferred_element_type=F32)
    frozen_t = jnp.swapaxes(frozen_query_projection, 1, 2)
    query_t = (frozen_t.astype(F32) + raised).astype(BF16)

    sizes = (per_question, slots_dev, span)
    stats, rows = attend_stats(chosen, query_t, upstream_t, key_table, value_table, *sizes)
    all_stats = to_all(stats, "tp")
    dq_parts, value_grads = query_value_grads(
        chosen, query_t, upstream_t, adapter_up_weight, all_stats, rows, group_count, *sizes
    )
    grads = key_grads(chosen, query_t, upstream_t, all_stats, rows, group_count, *sizes)
    value_back = exchange(value_grads, "grp")
    latent_grad_tile = jnp.sum(value_back[:, span:, :].astype(F32), axis=0).astype(BF16)
    grad_values = unpack(value_back, slots_dev, span)
    key_back = exchange(with_tile(grads, latent_grad_tile, span), "grp")
    grad_keys = unpack(key_back, slots_dev, span)
    latent_grad = untiled(key_back[:, span:, :], tiles).reshape(HEAD, questions, targets)
    grad_a = jnp.einsum("qdt,rqt->dr", hidden_t, latent_grad, preferred_element_type=F32)

    dq_t = scatter_sum_tp(dq_parts).astype(BF16).reshape(HEAD, questions, piece)
    adapted = jnp.transpose(dq_t, (1, 2, 0))
    start = lax.axis_index("tp") * piece
    latent_cut = lax.dynamic_slice_in_dim(latent_t, start, piece, 2)
    grad_b = jnp.einsum("rqt,dqt->rd", latent_cut, dq_t, preferred_element_type=F32)
    got = to_all(jnp.concatenate([grad_a, grad_b], axis=1), ("sect", "tp"))
    got, grad_keys = lax.optimization_barrier((got, grad_keys))
    grads = jnp.sum(got, axis=0)
    return (adapted, grad_keys, grad_values, grads[:, :HEAD], grads[:, HEAD:])


def solution(mesh):
    return jax.shard_map(
        local,
        mesh=mesh,
        in_specs=(
            P(("sect", "grp"), "tp", None),
            P(("sect", "grp"), "tp", None),
            P("sect", None, "grp"),
            P("sect", None, "grp"),
            P("sect", None, "grp"),
            P("grp", None),
            P(None, "grp"),
            P(("sect", "grp")),
            P(("sect", "grp")),
            P("sect"),
        ),
        out_specs=(
            P("sect", "tp", "grp"),
            P(("sect", "grp"), "tp", None),
            P(("sect", "grp"), "tp", None),
            P("grp", None),
            P(None, "grp"),
        ),
        check_vma=False,
    )
```
